32 devices in a mesh: tile: 8 (over z, x), lev: 4 (over y, core).
Axes of the slice: x: 2, y: 2, z: 4, core: 2. Of those that a mesh axis runs over, the one named last changes fastest.
Arguments:
- krylov: bfloat16 [4, 8, 5, 2048, 128], P(None, 'lev', None, 'tile'), may hold values from -7 to 7, as said below
- adjoint: float32 [8, 5, 2048, 128], P('lev', None, 'tile'), may hold values from -200 to 200
- projected: float32 [4, 4], replicated, may hold values from -3 to 3
- stencil: bfloat16 [5, 8, 2048, 128], P(None, 'lev', 'tile'), may hold values from 0.19921875 to 1
- column_weight: float32 [2, 8, 2048, 128], P(None, 'lev', 'tile'), may hold values from 0.05 to 0.3
- seam_turns: int32 [8, 4], P('tile'), may hold values from 0 to 3
Outputs:
- updated: float32 [8, 5, 2048, 128], P('lev', None, 'tile')
The draws below stay inside these ranges and needn't reach their ends.
Inputs may be any that keep to these rules, and one draw needn't show every extreme that they name: `krylov`: krylov vectors of order one.
All inputs are finite; a program needn't handle non-finite values.
Results may differ from the reference program's by a relative error of at most 0.0003.
Values sent between devices are 32-bit elements; how exact they have to be, the bound alone decides.
No kernel may reach another device: no remote copies, remote signals or barrier semaphores. Data moves between devices by JAX's collectives and lax.ppermute only.
A program may use at most 128 MiB of HBM per device.

```python
import math
import jax
import jax.numpy as jnp

FIELDS = 5
KRYLOV = 4
STRIDE = 4
HX = 256
HY = 128
TILES = 8
LEVELS = 8
ROWS = 2048


def shared_basis(key):
    return jax.random.normal(jax.random.fold_in(key, 11), (KRYLOV, LEVELS, FIELDS, ROWS, HY), jnp.float32)


def draw_krylov(key, part):
    return shared_basis(key).astype(jnp.bfloat16)


def draw_adjoint(key, part):
    basis_all = shared_basis(key)
    factors = jax.random.uniform(jax.random.fold_in(key, 12), (KRYLOV,), jnp.float32, -1.0, 1.0)
    blended = jnp.zeros((LEVELS, FIELDS, ROWS, HY), jnp.float32)
    for k in range(KRYLOV):
        blended = blended + 0.5 * factors[k] * basis_all[k]
    log_amp = jax.random.uniform(jax.random.fold_in(key, 14), (LEVELS, TILES), jnp.float32, -2.0794415, 2.0794415)
    amplitude = jnp.repeat(jnp.exp(log_amp), HX, axis=1)
    tile_rise = 1.0 + 2.0 * (jnp.arange(ROWS) // HX).astype(jnp.float32) / (TILES - 1)
    noise = jax.random.normal(jax.random.fold_in(key, 13), (LEVELS, FIELDS, ROWS, HY), jnp.float32)
    level_rise = 1.0 + 0.5 * jnp.arange(LEVELS).astype(jnp.float32) / (LEVELS - 1)
    rough = noise * tile_rise[None, None, :, None] * level_rise[:, None, None, None]
    return blended * amplitude[:, None, :, None] + rough


def with_ends(entries, stream_key, smallest, top_value):
    place = [jax.random.randint(jax.random.fold_in(stream_key, axis), (), 0, length) for axis, length in enumerate(entries.shape)]
    main_axis = entries.shape.index(max(entries.shape))
    neighbour = place[:main_axis] + [(place[main_axis] + 1) % entries.shape[main_axis]] + place[main_axis + 1:]
    return entries.at[tuple(place)].set(smallest).at[tuple(neighbour)].set(top_value)


def block_scale(rng, dims, shards, least, high):
    loudness = 1.0
    for position, blocks in shards:
        steps = jax.random.uniform(jax.random.fold_in(jax.random.fold_in(rng, 6), position), (blocks,), jnp.float32, least / len(shards), high / len(shards))
        loudness = loudness * jnp.repeat(jnp.exp(steps), dims[position] // blocks).reshape((-1,) + (1,) * (len(dims) - 1 - position))
    return loudness


def normal_values(stream_key, dims, deviation, limit, held_as=jnp.bfloat16):
    return jnp.clip(deviation * jax.random.normal(stream_key, dims, jnp.float32), -limit, limit).astype(held_as)


def setup_inputs(seed: int = 0) -> dict:
    arg_keys = jax.random.split(jax.random.key(seed), 7)
    krylov = draw_krylov(jax.random.fold_in(arg_keys[6], 71), 0)
    adjoint = draw_adjoint(jax.random.fold_in(arg_keys[6], 71), 0)
    projected = normal_values(arg_keys[2], (KRYLOV, KRYLOV), 1.0, 3.0, jnp.float32)
    stencil = jnp.clip(jnp.exp(math.log(1.0) - 1.6133518 * jax.random.uniform(arg_keys[3], (5, LEVELS, ROWS, HY), jnp.float32) ** block_scale(arg_keys[3], (5, LEVELS, ROWS, HY), ((1, 4), (2, 8)), -0.2, 0.2)), 0.19921875, 1.0).astype(jnp.bfloat16)
    column_weight = jnp.clip(jnp.exp(math.log(0.3) - 1.7917595 * jax.random.uniform(arg_keys[4], (2, LEVELS, ROWS, HY), jnp.float32) ** block_scale(arg_keys[4], (2, LEVELS, ROWS, HY), ((1, 4), (2, 8)), -0.2, 0.2)), 0.05, 0.3)
    seam_turns = with_ends(jax.random.randint(arg_keys[5], (TILES, 4), 0, 4), jax.random.fold_in(arg_keys[5], 1), 0, 3).astype(jnp.int32)
    return {"krylov": krylov, "adjoint": adjoint, "projected": projected, "stencil": stencil, "column_weight": column_weight, "seam_turns": seam_turns}


def rotate(edge_strip, turning):
    flipped = jnp.where(turning % 2 == 1, edge_strip[..., ::-1], edge_strip)
    cosine = jnp.where(turning == 0, 1.0, jnp.where(turning == 2, -1.0, 0.0)).astype(edge_strip.dtype)
    sine_part = jnp.where(turning == 1, 1.0, jnp.where(turning == 3, -1.0, 0.0)).astype(edge_strip.dtype)
    wind_east = flipped[..., 2:3, :]
    wind_north = flipped[..., 3:4, :]
    turned_u = cosine * wind_east - sine_part * wind_north
    turned_v = sine_part * wind_east + cosine * wind_north
    return jnp.concatenate([flipped[..., :2, :], turned_u, turned_v, flipped[..., 4:, :]], axis=-2)


def reference(krylov, adjoint, projected, stencil, column_weight, seam_turns):
    count = LEVELS * FIELDS * ROWS * HY
    coupling = jnp.stack([jnp.sum(krylov[k].astype(jnp.float32) * adjoint) for k in range(KRYLOV)]) / count
    mixing = jnp.sum(projected * coupling[:, None], axis=0)
    combined = jnp.zeros(adjoint.shape, jnp.float32)
    for k in range(KRYLOV):
        combined = combined + mixing[k] * krylov[k].astype(jnp.float32)
    field = jnp.transpose(combined.reshape(LEVELS, FIELDS, TILES, HX, HY), (2, 0, 1, 3, 4))
    coeffs = jnp.transpose(stencil.astype(jnp.float32).reshape(5, LEVELS, TILES, HX, HY), (0, 2, 1, 3, 4))[:, :, :, None]
    turning = [seam_turns[:, s][:, None, None, None] for s in range(4)]
    image = coeffs[0] * field
    plus_rows = coeffs[1] * field
    rim_strip = rotate(jnp.roll(plus_rows[..., -1, :], 1, axis=0), turning[0])
    image = image + jnp.concatenate([rim_strip[..., None, :], plus_rows[..., :-1, :]], axis=-2)
    minus_rows = coeffs[2] * field
    rim_strip = rotate(jnp.roll(minus_rows[..., 0, :], -1, axis=0), turning[1])
    image = image + jnp.concatenate([minus_rows[..., 1:, :], rim_strip[..., None, :]], axis=-2)
    plus_cols = coeffs[3] * field
    rim_strip = rotate(jnp.roll(plus_cols[..., -1], STRIDE, axis=0), turning[2])
    image = image + jnp.concatenate([rim_strip[..., None], plus_cols[..., :-1]], axis=-1)
    minus_cols = coeffs[4] * field
    rim_strip = rotate(jnp.roll(minus_cols[..., 0], -STRIDE, axis=0), turning[3])
    image = image + jnp.concatenate([minus_cols[..., 1:], rim_strip[..., None]], axis=-1)
    weights = jnp.transpose(column_weight.reshape(2, LEVELS, TILES, HX, HY), (0, 2, 1, 3, 4))
    pressure_sum = jnp.cumsum(field[:, ::-1, 0], axis=1)[:, ::-1]
    height_sum = jnp.cumsum(field[:, ::-1, 3], axis=1)[:, ::-1]
    zeros_part = jnp.zeros_like(pressure_sum)
    column_part = jnp.stack([zeros_part, weights[0] * pressure_sum, zeros_part, zeros_part, weights[1] * height_sum], axis=2)
    image = image + column_part
    image = jnp.transpose(image, (1, 2, 0, 3, 4)).reshape(LEVELS, FIELDS, ROWS, HY)
    return adjoint + 0.5 * image
```

```python
import functools

import jax
import jax.numpy as jnp
from jax import lax
from jax.experimental import pallas as pl
from jax.experimental.pallas import tpu as pltpu
from jax.sharding import PartitionSpec as P

STRIDE = 4
F32 = jnp.float32
VMEM_LIMIT = 24 * 1024 * 1024

ANY = pl.BlockSpec(memory_space=pl.ANY)
IN_VMEM = pl.BlockSpec(memory_space=pltpu.VMEM)
IN_SMEM = pl.BlockSpec(memory_space=pltpu.SMEM)


def pinned(x):
    return pltpu.with_memory_space_constraint(x, pltpu.VMEM)


def exchange(x, axis, bit):
    size = lax.axis_size(axis)
    return lax.ppermute(x, axis, [(i, i ^ bit) for i in range(size)])


def shifted(x, axis, steps):
    size = lax.axis_size(axis)
    return lax.ppermute(x, axis, [(i, (i + steps) % size) for i in range(size)])


def bits(axis):
    size = lax.axis_size(axis)
    return [1 << b for b in range(size.bit_length() - 1)]


def lanes(shape):
    return lax.broadcasted_iota(jnp.int32, shape, len(shape) - 1)


def rows(shape):
    return lax.broadcasted_iota(jnp.int32, shape, len(shape) - 2)


def dots_kernel(dims, core, kry, adj, kry_v, adj_v, part, mine, theirs, sums, sem_k, sem_a):
    vectors, levels, fields, height = dims
    half = vectors // 2
    order = [0, 3] + [f for f in range(fields) if f not in (0, 3)]
    copies = []
    for f in order:
        for l in range(levels):
            n = f * levels + l
            copies.append(
                (
                    f,
                    l,
                    pltpu.make_async_copy(kry.at[:, l, f], kry_v.at[:, l, f], sem_k.at[n]),
                    pltpu.make_async_copy(adj.at[l, f], adj_v.at[l, f], sem_a.at[n]),
                )
            )
    for _, _, a, b in copies:
        a.start()
        b.start()
    step = 32
    accs = [jnp.zeros((8, 128), F32) for _ in range(vectors)]
    for f, l, a, b in copies:
        a.wait()
        b.wait()

        def body(i, accs, f=f, l=l):
            at = pl.ds(pl.multiple_of(i * step, step), step)
            y = adj_v[l, f, at]
            out = []
            for k in range(vectors):
                x = kry_v[k, l, f, at].astype(F32)
                if f in (0, 3):
                    c = 0 if f == 0 else 1
                    if l == 0:
                        sums[k, c, at] = x
                    else:
                        sums[k, c, at] = sums[k, c, at] + x
                p = x * y
                out.append(accs[k] + jnp.sum(p.reshape(step // 8, 8, 128), axis=0))
            return out

        accs = lax.fori_loop(0, height // step, body, accs)
    low = core[0] == 0
    for k in range(half):

        @pl.when(low)
        def _(k=k):
            mine[k] = sums[k]
            theirs[k] = sums[half + k]

        @pl.when(jnp.logical_not(low))
        def _(k=k):
            mine[k] = sums[half + k]
            theirs[k] = sums[k]

    total = jnp.zeros((8, 128), F32)
    r = rows((8, 128))
    for k in range(vectors):
        total = jnp.where(r == k, jnp.sum(accs[k], axis=0, keepdims=True), total)
    part[...] = total


def strips_kernel(dims, kry_v, sten, cw, sten_v, cw_v, fwd, back, cols, sem):
    vectors, levels, fields, height = dims
    c1 = pltpu.make_async_copy(sten, sten_v, sem.at[0])
    c2 = pltpu.make_async_copy(cw, cw_v, sem.at[1])
    c1.start()
    c2.start()
    c1.wait()
    per = levels * fields
    fwd[...] = jnp.zeros_like(fwd)
    back[...] = jnp.zeros_like(back)
    tail = height - 16
    for l in range(levels):
        last = sten_v[1, l, tail:height].astype(F32)[15:16]
        first = sten_v[2, l, 0:16].astype(F32)[0:1]
        for k in range(vectors):
            for f in range(fields):
                s = k * 16 + l * fields + f
                fwd[s : s + 1] = kry_v[k, l, f, tail:height].astype(F32)[15:16] * last
                back[s : s + 1] = kry_v[k, l, f, 0:16].astype(F32)[0:1] * first
    step = 32

    def body(i, carry):
        at = pl.ds(pl.multiple_of(i * step, step), step)
        lane = lanes((step, 128))
        x = jnp.zeros((step, 128), F32)
        coeff = jnp.zeros((step, 128), F32)
        for l in range(levels):
            up = jnp.broadcast_to(sten_v[3, l, at].astype(F32)[:, 127:128], (step, 128))
            down = jnp.broadcast_to(sten_v[4, l, at].astype(F32)[:, 0:1], (step, 128))
            both = jnp.where(lane % 2 == 0, up, down)
            coeff = jnp.where(lane % (2 * per) // (2 * fields) == l, both, coeff)
            for k in range(vectors):
                for f in range(fields):
                    s = k * per + l * fields + f
                    moved = pltpu.roll(kry_v[k, l, f, at].astype(F32), 2 * s + 1, 1)
                    x = jnp.where(lane // 2 == s, moved, x)
        cols[at] = x * coeff
        return carry

    lax.fori_loop(0, height // step, body, 0)
    c2.wait()


def turn_of(r):
    cosine = jnp.where(r == 0, 1.0, jnp.where(r == 2, -1.0, 0.0)).astype(F32)
    sine = jnp.where(r == 1, 1.0, jnp.where(r == 3, -1.0, 0.0)).astype(F32)
    return cosine, sine


def turn_kernel(dims, turns, fwd, back, up, down, fwd_o, back_o, cols_o):
    vectors, levels, fields, height = dims
    per = levels * fields
    n = vectors * 16
    flip = (lanes((128, 128)) + rows((128, 128)) == 127).astype(F32)
    r = rows((n, 128)) % 16
    field = r % fields
    real = r < per
    for side, strip, out in ((0, fwd, fwd_o), (1, back, back_o)):
        turning = turns[0, side]
        x = strip[...]
        x = jnp.where(
            turning % 2 == 1,
            jnp.dot(x, flip, precision=lax.Precision.HIGHEST, preferred_element_type=F32),
            x,
        )
        cosine, sine = turn_of(turning)
        u = cosine * x - sine * pltpu.roll(x, n - 1, 0)
        v = sine * pltpu.roll(x, 1, 0) + cosine * x
        out[...] = jnp.where(real & (field == 2), u, jnp.where(real & (field == 3), v, x))
    lane = lanes((height, 128))
    even = lane % 2 == 0
    x = jnp.where(even, up[...], down[...])
    mirror = (lanes((height, height)) + rows((height, height)) == height - 1).astype(F32)
    mirrored = jnp.dot(mirror, x, precision=lax.Precision.HIGHEST, preferred_element_type=F32)
    t_up, t_down = turns[0, 2], turns[0, 3]
    odd = jnp.where(even, t_up % 2, t_down % 2)
    x = jnp.where(odd == 1, mirrored, x)
    cos_u, sin_u = turn_of(t_up)
    cos_d, sin_d = turn_of(t_down)
    cosine = jnp.where(even, cos_u, cos_d)
    sine = jnp.where(even, sin_u, sin_d)
    field = lane % (2 * fields) // 2
    u = cosine * x - sine * pltpu.roll(x, 126, 1)
    v = sine * pltpu.roll(x, 2, 1) + cosine * x
    x = jnp.where(field == 2, u, jnp.where(field == 3, v, x))
    cols_o[...] = jnp.where(even, pltpu.roll(x, 127, 1), pltpu.roll(x, 1, 1))


def final_kernel(
    dims, count, core, projected, part, kry, adj, sten, cw, fwd, back, cols, mine, other,
    out_hbm, comb, low, edges, rim_f, rim_b, out, sem,
):
    vectors, levels, fields, height = dims
    half = vectors // 2
    per = levels * fields
    coupling = [
        jnp.sum(part[k : k + 1], axis=1, keepdims=True) * (1.0 / count) for k in range(vectors)
    ]
    mix = []
    for j in range(vectors):
        m = projected[0, j] * coupling[0]
        for k in range(1, vectors):
            m = m + projected[k, j] * coupling[k]
        mix.append(m)
    is_low = core[0] == 0
    mine_mix = [jnp.where(is_low, mix[k], mix[half + k]) for k in range(half)]
    other_mix = [jnp.where(is_low, mix[half + k], mix[k]) for k in range(half)]

    rim_f[...] = sum(mix[k] * fwd[k * 16 : (k + 1) * 16] for k in range(vectors))
    rim_b[...] = sum(mix[k] * back[k * 16 : (k + 1) * 16] for k in range(vectors))

    step = 64
    chunks = height // step

    def combine(i, carry):
        at = pl.ds(pl.multiple_of(i * step, step), step)
        for c in range(2):
            low[c, at] = sum(
                mine_mix[k] * mine[k, c, at] + other_mix[k] * other[k, c, at] for k in range(half)
            )
        lane = lanes((step, 128)) // (2 * per)
        weight = jnp.zeros((step, 128), F32)
        for k in range(vectors):
            weight = jnp.where(lane == k, mix[k], weight)
        z = cols[at] * weight
        w = z
        for k in range(1, vectors):
            w = w + pltpu.roll(z, 128 - 2 * per * k, 1)
        edges[at] = w
        for l in range(levels):
            for f in range(fields):
                comb[l, f, at] = sum(mix[k] * kry[k, l, f, at].astype(F32) for k in range(vectors))
        return carry

    lax.fori_loop(0, chunks, combine, 0)

    copies = []
    for f in range(fields):

        def stencil(n, carry, f=f):
            l = n // chunks
            i = n % chunks
            at = pl.ds(pl.multiple_of(i * step, step), step)
            before = pl.ds(pl.multiple_of(jnp.maximum(i * step - 16, 0), 16), 16)
            after = pl.ds(pl.multiple_of(jnp.minimum(i * step + step, height - 16), 16), 16)
            q = l * fields + f
            x = comb[l, f, at]
            r = rows((step, 128))
            lane = lanes((step, 128))
            image = sten[0, l, at].astype(F32) * x
            p1 = sten[1, l, at].astype(F32) * x
            head = (sten[1, l, before].astype(F32) * comb[l, f, before])[15:16]
            head = jnp.where(i == 0, rim_f[pl.ds(q, 1)], head)
            image = image + jnp.where(r == 0, head, pltpu.roll(p1, 1, 0))
            p2 = sten[2, l, at].astype(F32) * x
            tail = (sten[2, l, after].astype(F32) * comb[l, f, after])[0:1]
            tail = jnp.where(i == chunks - 1, rim_b[pl.ds(q, 1)], tail)
            image = image + jnp.where(r == step - 1, tail, pltpu.roll(p2, step - 1, 0))
            side = pltpu.roll(edges[at], 127 - 2 * q, 1)
            p3 = sten[3, l, at].astype(F32) * x
            image = image + jnp.where(lane == 0, side, pltpu.roll(p3, 1, 1))
            p4 = sten[4, l, at].astype(F32) * x
            image = image + jnp.where(lane == 127, side, pltpu.roll(p4, 127, 1))
            if f in (1, 4):
                c, source = (0, 0) if f == 1 else (1, 3)
                column = low[c, at]
                for l2 in range(levels):
                    column = column + jnp.where(l2 >= l, comb[l2, source, at], 0.0)
                image = image + cw[c, l, at] * column
            out[l, f, at] = adj[l, f, at] + 0.5 * image
            return carry

        lax.fori_loop(0, levels * chunks, stencil, 0)
        copy = pltpu.make_async_copy(out.at[:, f], out_hbm.at[:, f], sem.at[f])
        copy.start()
        copies.append(copy)
    for copy in copies:
        copy.wait()


def per_device(krylov, adjoint, projected, stencil, column_weight, seam_turns):
    vectors, levels, fields, height, width = krylov.shape
    dims = (vectors, levels, fields, height)
    half = vectors // 2
    tiles, groups = lax.axis_size("tile"), lax.axis_size("lev")
    count = levels * fields * height * width * tiles * groups
    group = lax.axis_index("lev")
    core = (group % 2).astype(jnp.int32).reshape(1)
    params = pltpu.CompilerParams(vmem_limit_bytes=VMEM_LIMIT)
    bf16 = krylov.dtype

    kry, adj, part, mine, theirs = pl.pallas_call(
        functools.partial(dots_kernel, dims),
        out_shape=(
            pltpu.VMEM(krylov.shape, bf16),
            pltpu.VMEM(adjoint.shape, F32),
            pltpu.VMEM((8, 128), F32),
            pltpu.VMEM((half, 2, height, width), F32),
            pltpu.VMEM((half, 2, height, width), F32),
        ),
        in_specs=[IN_SMEM, ANY, ANY],
        out_specs=[IN_VMEM] * 5,
        scratch_shapes=[
            pltpu.VMEM((vectors, 2, height, width), F32),
            pltpu.SemaphoreType.DMA((levels * fields,)),
            pltpu.SemaphoreType.DMA((levels * fields,)),
        ],
        compiler_params=params,
        name="dots",
    )(core, krylov, adjoint)

    first = exchange(theirs, "lev", 1)
    segment = mine + first
    below = jnp.zeros_like(segment)
    for bit in bits("lev")[1:]:
        got = exchange(segment, "lev", bit)
        below = below + jnp.where(group & bit == 0, got, 0.0)
        segment = segment + got
    other = exchange(below + jnp.where(core == 1, mine, 0.0), "lev", 1)
    below = below + jnp.where(core == 0, first, 0.0)

    sten, cw, fwd, back, cols = pl.pallas_call(
        functools.partial(strips_kernel, dims),
        out_shape=(
            pltpu.VMEM(stencil.shape, stencil.dtype),
            pltpu.VMEM(column_weight.shape, F32),
            pltpu.VMEM((vectors * 16, width), F32),
            pltpu.VMEM((vectors * 16, width), F32),
            pltpu.VMEM((height, width), F32),
        ),
        in_specs=[IN_VMEM, ANY, ANY],
        out_specs=[IN_VMEM] * 5,
        scratch_shapes=[pltpu.SemaphoreType.DMA((2,))],
        compiler_params=params,
        name="strips",
    )(pinned(kry), stencil, column_weight)

    for bit in bits("lev")[1:]:
        part = part + exchange(part, "lev", bit)
    part = part + exchange(part, "lev", 1)
    for bit in bits("tile"):
        part = part + exchange(part, "tile", bit)

    up = shifted(cols, "tile", STRIDE)
    down = up if (2 * STRIDE) % tiles == 0 else shifted(cols, "tile", -STRIDE)
    fwd = shifted(fwd, "tile", 1)
    back = shifted(back, "tile", -1)
    fwd, back, cols = pl.pallas_call(
        functools.partial(turn_kernel, dims),
        out_shape=(
            pltpu.VMEM(fwd.shape, F32),
            pltpu.VMEM(back.shape, F32),
            pltpu.VMEM(cols.shape, F32),
        ),
        in_specs=[IN_SMEM] + [IN_VMEM] * 4,
        out_specs=[IN_VMEM] * 3,
        compiler_params=params,
        name="turn",
    )(seam_turns, pinned(fwd), pinned(back), pinned(up), pinned(down))

    return pl.pallas_call(
        functools.partial(final_kernel, dims, count),
        out_shape=jax.ShapeDtypeStruct(adjoint.shape, F32),
        in_specs=[IN_SMEM, IN_SMEM] + [IN_VMEM] * 10,
        out_specs=ANY,
        scratch_shapes=[
            pltpu.VMEM((levels, fields, height, width), F32),
            pltpu.VMEM((2, height, width), F32),
            pltpu.VMEM((height, width), F32),
            pltpu.VMEM((16, width), F32),
            pltpu.VMEM((16, width), F32),
            pltpu.VMEM((levels, fields, height, width), F32),
            pltpu.SemaphoreType.DMA((fields,)),
        ],
        compiler_params=params,
        name="final",
    )(
        core, projected, pinned(part), pinned(kry), pinned(adj), pinned(sten), pinned(cw),
        pinned(fwd), pinned(back), pinned(cols), pinned(below), pinned(other),
    )


def solution(mesh):
    placed = (
        P(None, "lev", None, "tile", None),
        P("lev", None, "tile", None),
        P(),
        P(None, "lev", "tile", None),
        P(None, "lev", "tile", None),
        P("tile", None),
    )
    return jax.shard_map(
        per_device,
        mesh=mesh,
        in_specs=placed,
        out_specs=P("lev", None, "tile", None),
        check_vma=False,
    )
```

```python
import functools

import jax
import jax.numpy as jnp
from jax import lax
from jax.experimental import pallas as pl
from jax.experimental.pallas import tpu as pltpu
from jax.sharding import PartitionSpec as P

STRIDE = 4
F32 = jnp.float32
SMALL = 4 * 1024 * 1024
LARGE = 8 * 1024 * 1024

IN_HBM = pl.BlockSpec(memory_space=pltpu.HBM)
IN_VMEM = pl.BlockSpec(memory_space=pltpu.VMEM)


def pinned(x):
    return pltpu.with_memory_space_constraint(x, pltpu.VMEM)


def in_hbm(x):
    return pltpu.with_memory_space_constraint(x, pltpu.HBM)


def exchange(x, axis, bit):
    size = lax.axis_size(axis)
    return lax.ppermute(x, axis, [(i, i ^ bit) for i in range(size)])


def shifted(x, axis, steps):
    size = lax.axis_size(axis)
    return lax.ppermute(x, axis, [(i, (i + steps) % size) for i in range(size)])


def bits(axis):
    size = lax.axis_size(axis)
    return [1 << b for b in range(size.bit_length() - 1)]


def lanes(shape):
    return lax.broadcasted_iota(jnp.int32, shape, len(shape) - 1)


def rows(shape):
    return lax.broadcasted_iota(jnp.int32, shape, len(shape) - 2)


def bf16(x):
    return x.astype(jnp.bfloat16)


def ends_to(last, first):
    row, lane = rows((16, 128)), lanes((16, 128))
    top = bf16(jnp.where((row == 0) & first(lane), 1.0, 0.0))
    bottom = bf16(jnp.where((row == 15) & last(lane), 1.0, 0.0))
    return jnp.concatenate([top, jnp.zeros((96, 128), jnp.bfloat16), bottom], axis=0)


def dots_kernel(
    dims, count, projected, kry, adj, kry_v, pack, mine, adj_v, proj_v, mixer, sem_k, sem_a, sem_p
):
    vectors, levels, fields, height = dims
    half = vectors // 2
    upper = lax.axis_index("lev") & 1 == 1
    order = [0, 3] + [f for f in range(fields) if f not in (0, 3)]
    copy_p = pltpu.make_async_copy(projected, proj_v, sem_p)
    copy_p.start()
    copies = {}
    for f in order:
        copies[f] = (
            pltpu.make_async_copy(kry.at[:, :, f], kry_v.at[:, :, f], sem_k.at[f]),
            pltpu.make_async_copy(adj.at[:, f], adj_v.at[:, f], sem_a.at[f]),
        )
        for copy in copies[f]:
            copy.start()
    copy_p.wait()
    r = rows((8, 128))
    for k in range(vectors):
        m = jnp.zeros((8, 128), F32)
        for j in range(vectors):
            m = jnp.where(r == j, proj_v[k : k + 1, j : j + 1] * (0.5 / count), m)
        mixer[k] = m
    step = 128
    accs = [jnp.zeros((8, 128), F32) for _ in range(vectors)]
    for f in order:
        for copy in copies[f]:
            copy.wait()
        for l in range(levels):

            def body(i, accs, f=f, l=l):
                start = pl.multiple_of(i * step, step)
                at = pl.ds(start, step)
                y = adj_v[l, f, at]
                out = []
                for k in range(vectors):
                    x = kry_v[k, l, f, at].astype(F32)
                    if f in (0, 3):
                        c = 0 if f == 0 else 1
                        to = pl.ds(start + ((k % half) * 2 + c) * height, step)

                        def put(ref, x=x, to=to):
                            if l == 0:
                                ref[to] = x
                            else:
                                ref[to] = ref[to] + x

                        first, second = (mine, pack) if k < half else (pack, mine)
                        pl.when(jnp.logical_not(upper))(functools.partial(put, first))
                        pl.when(upper)(functools.partial(put, second))
                    p = x * y
                    out.append(accs[k] + jnp.sum(p.reshape(step // 8, 8, 128), axis=0))
                return out

            accs = lax.fori_loop(0, height // step, body, accs)
    total = jnp.zeros((8, 128), F32)
    for k in range(vectors):
        total = total + mixer[k] * jnp.sum(accs[k], axis=0, keepdims=True)
    pack[vectors * height : vectors * height + 8] = total


def strips_kernel(dims, kry_v, sten, sten_v, near, far, cols, sem):
    vectors, levels, fields, height = dims
    per = levels * fields
    even_tile = lax.axis_index("tile") & 1 == 0
    copy = pltpu.make_async_copy(sten, sten_v, sem)
    copy.start()
    near[...] = jnp.zeros_like(near)
    far[...] = jnp.zeros_like(far)
    planes = [(k, l, f) for k in range(vectors) for l in range(levels) for f in range(fields)]
    cols[...] = jnp.dot(
        jnp.concatenate([kry_v[p] for p in planes], axis=1),
        jnp.concatenate(
            [
                ends_to(lambda lane, s=2 * s: lane == s, lambda lane, s=2 * s: lane == s + 1)
                for s in range(len(planes))
            ],
            axis=0,
        ),
        preferred_element_type=F32,
    )
    copy.wait()
    tail = height - 16
    for l in range(levels):
        last = sten_v[1, l, tail:height].astype(F32)
        first = sten_v[2, l, 0:16].astype(F32)
        for k in range(vectors):
            for f in range(fields):
                s = k * 16 + l * fields + f
                fwd = (kry_v[k, l, f, tail:height].astype(F32) * last)[15:16]
                back = (kry_v[k, l, f, 0:16].astype(F32) * first)[0:1]
                near[8 + s : 9 + s] = jnp.where(even_tile, fwd, back)
                far[s : s + 1] = jnp.where(even_tile, back, fwd)
    none = lambda lane: lane < 0
    weights = []
    for l in range(levels):
        here = lambda lane, l=l: lane % (2 * per) // (2 * fields) == l
        weights.append(ends_to(lambda lane, here=here: here(lane) & (lane % 2 == 0), none))
        weights.append(ends_to(none, lambda lane, here=here: here(lane) & (lane % 2 == 1)))
    coeff = jnp.dot(
        jnp.concatenate([sten_v[d, l] for l in range(levels) for d in (3, 4)], axis=1),
        jnp.concatenate(weights, axis=0),
        preferred_element_type=F32,
    )
    cols[...] = cols[...] * coeff


def turn_of(r):
    cosine = jnp.where(r == 0, 1.0, jnp.where(r == 2, -1.0, 0.0)).astype(F32)
    sine = jnp.where(r == 1, 1.0, jnp.where(r == 3, -1.0, 0.0)).astype(F32)
    return cosine, sine


def turn_kernel(dims, turns, near, far, up, down, fwd_o, back_o, cols_o):
    vectors, levels, fields, height = dims
    per = levels * fields
    n = vectors * 16
    flip = (lanes((128, 128)) + rows((128, 128)) == 127).astype(F32)
    r = rows((n, 128)) % 16
    field = r % fields
    real = r < per
    even_tile = lax.axis_index("tile") & 1 == 0
    for side, out in ((0, fwd_o), (1, back_o)):
        turning = jnp.broadcast_to(turns[0:1, side : side + 1], (n, 128))
        first, second = (far[...], near[8:]) if side == 0 else (near[8:], far[...])
        x = jnp.where(even_tile, first, second)
        x = jnp.where(
            turning % 2 == 1,
            jnp.dot(x, flip, precision=lax.Precision.HIGHEST, preferred_element_type=F32),
            x,
        )
        cosine, sine = turn_of(turning)
        u = cosine * x - sine * pltpu.roll(x, n - 1, 0)
        v = sine * pltpu.roll(x, 1, 0) + cosine * x
        out[...] = jnp.where(real & (field == 2), u, jnp.where(real & (field == 3), v, x))
    lane = lanes((height, 128))
    even = lane % 2 == 0
    x = jnp.where(even, up[...], down[...])
    mirror = (lanes((height, height)) + rows((height, height)) == height - 1).astype(F32)
    mirrored = jnp.dot(mirror, x, precision=lax.Precision.HIGHEST, preferred_element_type=F32)
    turning = jnp.where(lanes((1, 128)) % 2 == 0, turns[0:1, 2:3], turns[0:1, 3:4])
    x = jnp.where(turning % 2 == 1, mirrored, x)
    cosine, sine = turn_of(turning)
    field = lane % (2 * fields) // 2
    u = cosine * x - sine * pltpu.roll(x, 126, 1)
    v = sine * pltpu.roll(x, 2, 1) + cosine * x
    cols_o[...] = jnp.where(field == 2, u, jnp.where(field == 3, v, x))


def tables_kernel(dims, sten, cw, token, coefs, shift, spots, cw_v, sem):
    del token
    vectors, levels, fields, height = dims
    per = levels * fields
    copy = pltpu.make_async_copy(cw, cw_v, sem)
    copy.start()
    row, lane = rows((128, 256)), lanes((128, 256))
    move = bf16(jnp.where((lane == row + 1) & (row < 127) | (lane == row + 127) & (row > 0), 1.0, 0.0))
    shift[0:128] = move
    shift[128:256] = move
    source = row % (2 * per)
    for q in range(per):
        hit = (source == 2 * q) & (lane == 0) | (source == 2 * q + 1) & (lane == 255)
        spot = bf16(jnp.where(hit & (row < 2 * per * vectors), 1.0, 0.0))
        spots[q, 0:128] = spot
        spots[q, 128:256] = spot
    one = jnp.ones((1, 128), F32)
    lane = lanes((height, 128))
    for l in range(levels):
        coefs[0, l] = bf16(jnp.concatenate([one, sten[1, l].astype(F32)[:-1]], axis=0))
        coefs[1, l] = bf16(jnp.concatenate([sten[2, l].astype(F32)[1:], one], axis=0))
        right = jnp.dot(sten[3, l], move[:, 0:128], preferred_element_type=F32)
        left = jnp.dot(sten[4, l], move[:, 128:256], preferred_element_type=F32)
        coefs[2, l] = bf16(jnp.where(lane == 0, 1.0, right))
        coefs[3, l] = bf16(jnp.where(lane == 127, 1.0, left))
    copy.wait()


def split(x):
    high = bf16(x)
    return jnp.concatenate([high, bf16(x - high.astype(F32))], axis=1)


def final_kernel(
    dims, part, kry, adj, sten, coefs, shift, spots, cw, fwd, back, cols, mine, other,
    out_hbm, comb, low, edges, moved, out, sem,
):
    vectors, levels, fields, height = dims
    half = vectors // 2
    per = levels * fields
    total = jnp.broadcast_to(jnp.sum(part[...], axis=1, keepdims=True), (8, 128))
    mix = [jnp.broadcast_to(total[j : j + 1], (8, 128)) for j in range(vectors)]
    is_low = lax.axis_index("lev") & 1 == 0
    mine_mix = [jnp.where(is_low, mix[k], mix[half + k]) for k in range(half)]
    other_mix = [jnp.where(is_low, mix[half + k], mix[k]) for k in range(half)]

    def times(m, x):
        return (x.reshape(-1, 8, 128) * m).reshape(x.shape)

    rim_f = sum(times(mix[k], fwd[k * 16 : (k + 1) * 16]) for k in range(vectors))
    rim_b = sum(times(mix[k], back[k * 16 : (k + 1) * 16]) for k in range(vectors))
    for q in range(per):
        comb[q, 7:8] = rim_f[q : q + 1]
        comb[q, 8 + height : 9 + height] = rim_b[q : q + 1]

    lane = lanes((8, 128)) // (2 * per)
    weight = jnp.zeros((8, 128), F32)
    for k in range(vectors):
        weight = jnp.where(lane == k, mix[k], weight)
    step = 64
    for i in range(height // step):
        edges[i * step : (i + 1) * step] = split(times(weight, cols[i * step : (i + 1) * step]))

    def combine(l, f):
        for i in range(height // step):
            at = slice(i * step, (i + 1) * step)
            comb[l * fields + f, 8 + i * step : 8 + (i + 1) * step] = sum(
                times(mix[k], kry[k, l, f, at].astype(F32)) for k in range(vectors)
            )

    def column(c):
        for i in range(height // step):
            at = slice(i * step, (i + 1) * step)
            x = 0.0
            for k in range(half):
                here = slice((k * 2 + c) * height + i * step, (k * 2 + c) * height + (i + 1) * step)
                x = x + (times(mine_mix[k], mine[here]) + times(other_mix[k], other[here]))
            for l in reversed(range(levels)):
                q = l * fields + (0 if c == 0 else 3)
                x = x + comb[q, 8 + i * step : 8 + (i + 1) * step]
                low[c, l, at] = cw[c, l, at] * x

    def move(l, f):
        q = l * fields + f
        x = comb[q, 8 : 8 + height]
        moved[q % 2] = jnp.dot(split(x), shift[...], preferred_element_type=F32) + jnp.dot(
            edges[...], spots[q], preferred_element_type=F32
        )

    def stencil(l, f):
        q = l * fields + f
        for i in range(height // step):
            at = slice(i * step, (i + 1) * step)
            first = 8 + i * step
            image = (
                sten[0, l, at].astype(F32) * comb[q, first : first + step]
                + coefs[0, l, at].astype(F32) * comb[q, first - 1 : first + step - 1]
                + coefs[1, l, at].astype(F32) * comb[q, first + 1 : first + step + 1]
                + coefs[2, l, at].astype(F32) * moved[q % 2, at, 0:128]
                + coefs[3, l, at].astype(F32) * moved[q % 2, at, 128:256]
            )
            if f in (1, 4):
                image = image + low[0 if f == 1 else 1, l, at]
            out[l, f, at] = adj[l, f, at] + image

    order = [0, 3] + [f for f in range(fields) if f not in (0, 3)]
    planes = [(l, f) for f in order for l in range(levels)]
    combine(*planes[0])
    copies = []
    for n, (l, f) in enumerate(planes):
        if n + 1 < len(planes):
            combine(*planes[n + 1])
        if n == 2 * levels - 1:
            column(0)
            column(1)
        move(l, f)
        stencil(l, f)
        copy = pltpu.make_async_copy(out.at[l, f], out_hbm.at[l, f], sem.at[n])
        copy.start()
        copies.append(copy)
    for copy in copies:
        copy.wait()


def final_scratch(dims):
    _, levels, fields, height = dims
    return [
        pltpu.VMEM((levels * fields, height + 16, 128), F32),
        pltpu.VMEM((2, levels, height, 128), F32),
        pltpu.VMEM((height, 256), jnp.bfloat16),
        pltpu.VMEM((2, height, 256), F32),
        pltpu.VMEM((levels, fields, height, 128), F32),
        pltpu.SemaphoreType.DMA((levels * fields,)),
    ]


def pair_kernel(pack, got, o):
    o[...] = pack[-8:] + got[-8:]


def segment_kernel(got, mine, token, held, o):
    del token, held
    o[...] = mine[...] + got[0 : o.shape[0]]


def join_kernel(a, b, near, o):
    del near
    o[0:8] = a[...] + b[...]


def add_kernel(a, b, o):
    o[...] = a[0:8] + b[0:8]


def keep_kernel(x, token, held, o):
    del token, held
    o[...] = x[...]


def after(x, token, held):
    return local(
        keep_kernel,
        "after",
        50,
        pltpu.VMEM(x.shape, F32),
        [IN_VMEM] * 3,
        *map(pinned, (x, token, held)),
    )


def below_kernel(group_bits, got, mine, token, held, *refs):
    del token, held
    above, (send_o, mine_o) = refs[:-2], refs[-2:]
    group = lax.axis_index("lev")
    upper = group & 1 == 1
    split = mine.shape[0]
    step = 256

    def body(i, carry):
        at = pl.ds(pl.multiple_of(i * step, step), step)
        x = jnp.zeros((step, 128), F32)
        for bit, ref in zip(group_bits, above, strict=True):
            x = x + jnp.where(group & bit == 0, ref[at], 0.0)
        send_o[at] = x + jnp.where(upper, mine[at], 0.0)
        mine_o[at] = x + jnp.where(upper, 0.0, got[at])
        return carry

    lax.fori_loop(0, split // step, body, 0)


def local(kernel, name, us, out_shape, in_specs, *args, limit=SMALL, **more):
    return pl.pallas_call(
        kernel,
        out_shape=out_shape,
        in_specs=in_specs,
        out_specs=jax.tree.map(lambda _: IN_VMEM, out_shape),
        compiler_params=pltpu.CompilerParams(vmem_limit_bytes=limit),
        cost_estimate=pl.CostEstimate(
            flops=int(us * 1e9), bytes_accessed=int(us * 3.5e6), transcendentals=0
        ),
        name=name,
        **more,
    )(*args)


def add(a, b):
    return local(
        add_kernel, "add", 50, pltpu.VMEM((8, 128), F32), [IN_VMEM] * 2, pinned(a), pinned(b)
    )


def per_device(krylov, adjoint, projected, stencil, column_weight, seam_turns):
    vectors, levels, fields, height, width = krylov.shape
    dims = (vectors, levels, fields, height)
    half, per = vectors // 2, levels * fields
    tiles, groups = lax.axis_size("tile"), lax.axis_size("lev")
    count = levels * fields * height * width * tiles * groups
    total_rows = vectors * height
    bf = krylov.dtype
    dma = pltpu.SemaphoreType.DMA

    kry, pack, mine, adj = local(
        functools.partial(dots_kernel, dims, count),
        "dots",
        2,
        (
            pltpu.VMEM(krylov.shape, bf),
            pltpu.VMEM((total_rows + 8, width), F32),
            pltpu.VMEM((total_rows, width), F32),
            pltpu.VMEM(adjoint.shape, F32),
        ),
        [IN_HBM] * 3,
        *map(in_hbm, (projected, krylov, adjoint)),
        scratch_shapes=[
            pltpu.VMEM(projected.shape, F32),
            pltpu.VMEM((vectors, 8, 128), F32),
            dma((fields,)),
            dma((fields,)),
            dma,
        ],
    )
    sten, near, far, cols = local(
        functools.partial(strips_kernel, dims),
        "strips",
        1.5,
        (
            pltpu.VMEM(stencil.shape, bf),
            pltpu.VMEM((vectors * 16 + 8, width), F32),
            pltpu.VMEM((vectors * 16, width), F32),
            pltpu.VMEM((height, width), F32),
        ),
        [IN_VMEM, IN_HBM],
        pinned(kry),
        in_hbm(stencil),
        scratch_shapes=[dma],
    )

    first = exchange(pack, "lev", 1)
    part = local(
        pair_kernel, "pair", 0.1, pltpu.VMEM((8, width), F32), [IN_VMEM] * 2, pinned(pack), pinned(first)
    )
    segment = local(
        segment_kernel,
        "segment",
        50,
        pltpu.VMEM(mine.shape, F32),
        [IN_VMEM] * 4,
        *map(pinned, (first, mine, part, kry)),
    )
    above = []
    for bit in bits("lev")[1:]:
        if above:
            segment = segment + above[-1]
        above.append(exchange(segment, "lev", bit))
    cols = after(cols, part, kry)
    up = shifted(cols, "tile", STRIDE)
    down = up if (2 * STRIDE) % tiles == 0 else shifted(cols, "tile", -STRIDE)

    for bit in bits("lev")[1:-1]:
        part = add(part, exchange(part, "lev", bit))
    got = exchange(part, "lev", bits("lev")[-1])
    near = local(
        join_kernel,
        "join",
        50,
        pltpu.VMEM(near.shape, F32),
        [IN_VMEM] * 3,
        *map(pinned, (part, got, near)),
        input_output_aliases={2: 0},
    )
    far = after(far, near, kry)
    got = exchange(near, "tile", 1)
    part = add(near, got)
    near = got
    far = lax.ppermute(
        far, "tile", [(i, (i + 1 if i % 2 else i - 1) % tiles) for i in range(tiles)]
    )
    for bit in bits("tile")[1:-1]:
        part = add(part, exchange(part, "tile", bit))
    token = part
    for bit in bits("tile")[-1:]:
        part = add(part, exchange(part, "tile", bit))

    send, mine = local(
        functools.partial(below_kernel, bits("lev")[1:]),
        "below",
        50,
        (pltpu.VMEM(mine.shape, F32), pltpu.VMEM(mine.shape, F32)),
        [IN_VMEM] * (4 + len(above)),
        *map(pinned, (first, mine, token, kry, *above)),
    )
    other = exchange(send, "lev", 1)

    coefs, shift, spots, cw = local(
        functools.partial(tables_kernel, dims),
        "tables",
        1.5,
        (
            pltpu.VMEM((4,) + stencil.shape[1:], bf),
            pltpu.VMEM((256, 256), bf),
            pltpu.VMEM((per, 256, 256), bf),
            pltpu.VMEM(column_weight.shape, F32),
        ),
        [IN_VMEM, IN_HBM, IN_VMEM],
        pinned(sten),
        in_hbm(column_weight),
        pinned(token),
        scratch_shapes=[dma],
    )
    fwd, back, cols = local(
        functools.partial(turn_kernel, dims),
        "turn",
        1,
        (
            pltpu.VMEM(far.shape, F32),
            pltpu.VMEM(far.shape, F32),
            pltpu.VMEM(cols.shape, F32),
        ),
        [IN_VMEM] * 5,
        *map(pinned, (seam_turns, near, far, up, down)),
    )

    return pl.pallas_call(
        functools.partial(final_kernel, dims),
        out_shape=jax.ShapeDtypeStruct(adjoint.shape, F32),
        in_specs=[IN_VMEM] * 13,
        out_specs=IN_HBM,
        scratch_shapes=final_scratch(dims),
        compiler_params=pltpu.CompilerParams(vmem_limit_bytes=LARGE),
        name="final",
    )(
        *map(
            pinned,
            (part, kry, adj, sten, coefs, shift, spots, cw, fwd, back, cols, mine, other),
        )
    )


def solution(mesh):
    placed = (
        P(None, "lev", None, "tile", None),
        P("lev", None, "tile", None),
        P(),
        P(None, "lev", "tile", None),
        P(None, "lev", "tile", None),
        P("tile", None),
    )
    return jax.shard_map(
        per_device,
        mesh=mesh,
        in_specs=placed,
        out_specs=P("lev", None, "tile", None),
        check_vma=False,
    )
```

```python
import functools

import jax
import jax.numpy as jnp
from jax import lax
from jax.experimental import pallas as pl
from jax.experimental.pallas import tpu as pltpu
from jax.sharding import PartitionSpec as P

STRIDE = 4
F32 = jnp.float32
SMALL = 4 * 1024 * 1024
LARGE = 8 * 1024 * 1024

IN_HBM = pl.BlockSpec(memory_space=pltpu.HBM)
IN_VMEM = pl.BlockSpec(memory_space=pltpu.VMEM)


def pinned(x):
    return pltpu.with_memory_space_constraint(x, pltpu.VMEM)


def in_hbm(x):
    return pltpu.with_memory_space_constraint(x, pltpu.HBM)


def exchange(x, axis, bit):
    size = lax.axis_size(axis)
    return lax.ppermute(x, axis, [(i, i ^ bit) for i in range(size)])


def shifted(x, axis, steps):
    size = lax.axis_size(axis)
    return lax.ppermute(x, axis, [(i, (i + steps) % size) for i in range(size)])


def bits(axis):
    size = lax.axis_size(axis)
    return [1 << b for b in range(size.bit_length() - 1)]


def lanes(shape):
    return lax.broadcasted_iota(jnp.int32, shape, len(shape) - 1)


def rows(shape):
    return lax.broadcasted_iota(jnp.int32, shape, len(shape) - 2)


def bf16(x):
    return x.astype(jnp.bfloat16)


def split(x):
    high = bf16(x)
    return jnp.concatenate([high, bf16(x - high.astype(F32))], axis=1)


def ends_to(last, first):
    row, lane = rows((16, 128)), lanes((16, 128))
    top = bf16(jnp.where((row == 0) & first(lane), 1.0, 0.0))
    bottom = bf16(jnp.where((row == 15) & last(lane), 1.0, 0.0))
    return jnp.concatenate([top, jnp.zeros((96, 128), jnp.bfloat16), bottom], axis=0)


def dots_kernel(
    dims, count, projected, kry, adj, kry_v, pack, mine, adj_v, proj_v, mixer, sem_k, sem_a, sem_p
):
    vectors, levels, fields, height = dims
    half = vectors // 2
    upper = lax.axis_index("lev") & 1 == 1
    order = [0, 3] + [f for f in range(fields) if f not in (0, 3)]
    copy_p = pltpu.make_async_copy(projected, proj_v, sem_p)
    copy_p.start()
    copies = {}
    for f in order:
        copies[f] = (
            pltpu.make_async_copy(kry.at[:, :, f], kry_v.at[:, :, f], sem_k.at[f]),
            pltpu.make_async_copy(adj.at[:, f], adj_v.at[:, f], sem_a.at[f]),
        )
        for copy in copies[f]:
            copy.start()
    step = 128
    accs = [jnp.zeros((8, 128), F32) for _ in range(vectors)]
    for f in order:
        for copy in copies[f]:
            copy.wait()
        for l in range(levels):

            def body(i, accs, f=f, l=l):
                start = pl.multiple_of(i * step, step)
                at = pl.ds(start, step)
                y = adj_v[l, f, at]
                xs = [kry_v[k, l, f, at].astype(F32) for k in range(vectors)]
                if f in (0, 3):
                    for k in range(half):
                        to = pl.ds(start + (k * 2 + (0 if f == 0 else 1)) * height, step)
                        a, b = xs[k], xs[half + k]
                        for ref, x in ((mine, jnp.where(upper, b, a)), (pack, jnp.where(upper, a, b))):
                            ref[to] = x if l == 0 else ref[to] + x
                out = [
                    acc + jnp.sum((x * y).reshape(step // 8, 8, 128), axis=0)
                    for acc, x in zip(accs, xs, strict=True)
                ]
                return out

            accs = lax.fori_loop(0, height // step, body, accs)
    copy_p.wait()
    r = rows((8, 128))
    for k in range(vectors):
        m = jnp.zeros((8, 128), F32)
        for j in range(vectors):
            m = jnp.where(r == j, proj_v[k : k + 1, j : j + 1] * (0.5 / count), m)
        mixer[k] = m
    total = jnp.zeros((8, 128), F32)
    for k in range(vectors):
        total = total + mixer[k] * jnp.sum(accs[k], axis=0, keepdims=True)
    pack[vectors * height : vectors * height + 8] = total


def strips_kernel(dims, kry_v, sten, sten_v, near, far, cols_t, cols, sem):
    vectors, levels, fields, height = dims
    per = levels * fields
    even_tile = lax.axis_index("tile") & 1 == 0
    copy = pltpu.make_async_copy(sten, sten_v, sem)
    copy.start()
    near[...] = jnp.zeros_like(near)
    far[...] = jnp.zeros_like(far)
    planes = [(k, l, f) for k in range(vectors) for l in range(levels) for f in range(fields)]
    cols[...] = jnp.dot(
        jnp.concatenate([kry_v[p] for p in planes], axis=1),
        jnp.concatenate(
            [
                ends_to(lambda lane, s=2 * s: lane == s, lambda lane, s=2 * s: lane == s + 1)
                for s in range(len(planes))
            ],
            axis=0,
        ),
        preferred_element_type=F32,
    )
    copy.wait()
    tail = height - 16
    for l in range(levels):
        last = sten_v[1, l, tail:height].astype(F32)
        first = sten_v[2, l, 0:16].astype(F32)
        for k in range(vectors):
            for f in range(fields):
                s = k * 16 + l * fields + f
                fwd = (kry_v[k, l, f, tail:height].astype(F32) * last)[15:16]
                back = (kry_v[k, l, f, 0:16].astype(F32) * first)[0:1]
                near[8 + s : 9 + s] = jnp.where(even_tile, fwd, back)
                far[s : s + 1] = jnp.where(even_tile, back, fwd)
    none = lambda lane: lane < 0
    weights = []
    for l in range(levels):
        here = lambda lane, l=l: lane % (2 * per) // (2 * fields) == l
        weights.append(ends_to(lambda lane, here=here: here(lane) & (lane % 2 == 0), none))
        weights.append(ends_to(none, lambda lane, here=here: here(lane) & (lane % 2 == 1)))
    coeff = jnp.dot(
        jnp.concatenate([sten_v[d, l] for l in range(levels) for d in (3, 4)], axis=1),
        jnp.concatenate(weights, axis=0),
        preferred_element_type=F32,
    )
    cols_t[...] = jnp.transpose(cols[...] * coeff)[0 : cols_t.shape[0]]


def turn_of(r):
    cosine = jnp.where(r == 0, 1.0, jnp.where(r == 2, -1.0, 0.0)).astype(F32)
    sine = jnp.where(r == 1, 1.0, jnp.where(r == 3, -1.0, 0.0)).astype(F32)
    return cosine, sine


def turn_kernel(dims, turns, near, far, up, down, fwd_o, back_o, cols_o):
    vectors, levels, fields, height = dims
    per = levels * fields
    n = vectors * 16
    flip = bf16(jnp.where(lanes((128, 128)) + rows((128, 128)) == 127, 1.0, 0.0))
    flip = jnp.concatenate([flip, flip], axis=0)
    r = rows((n, 128)) % 16
    field = r % fields
    real = r < per
    even_tile = lax.axis_index("tile") & 1 == 0
    for side, out in ((0, fwd_o), (1, back_o)):
        turning = jnp.broadcast_to(turns[0:1, side : side + 1], (n, 128))
        first, second = (far[...], near[8:]) if side == 0 else (near[8:], far[...])
        x = jnp.where(even_tile, first, second)
        x = jnp.where(
            turning % 2 == 1,
            jnp.dot(split(x), flip, preferred_element_type=F32),
            x,
        )
        cosine, sine = turn_of(turning)
        u = cosine * x - sine * pltpu.roll(x, n - 1, 0)
        v = sine * pltpu.roll(x, 1, 0) + cosine * x
        out[...] = jnp.where(real & (field == 2), u, jnp.where(real & (field == 3), v, x))
    strips = up.shape[0]
    r = rows((strips, 1))
    even = r % 2 == 0
    x = jnp.where(even, up[...], down[...])
    mirror = bf16(jnp.where(lanes((height, height)) + rows((height, height)) == height - 1, 1.0, 0.0))
    mirrored = jnp.dot(
        split(x), jnp.concatenate([mirror, mirror], axis=0), preferred_element_type=F32
    )
    turning = jnp.where(even, turns[0:1, 2:3], turns[0:1, 3:4])
    x = jnp.where(turning % 2 == 1, mirrored, x)
    cosine, sine = turn_of(turning)
    field = r % (2 * fields) // 2
    u = cosine * x - sine * pltpu.roll(x, strips - 2, 0)
    v = sine * pltpu.roll(x, 2, 0) + cosine * x
    x = jnp.where(field == 2, u, jnp.where(field == 3, v, x))
    cols_o[...] = jnp.transpose(
        jnp.concatenate([x, jnp.zeros((128 - strips, height), F32)], axis=0)
    )


def tables_kernel(dims, sten, cw, token, coefs, shift, spots, cw_v, sem):
    del token
    vectors, levels, fields, height = dims
    per = levels * fields
    copy = pltpu.make_async_copy(cw, cw_v, sem)
    copy.start()
    row, lane = rows((128, 256)), lanes((128, 256))
    move = bf16(jnp.where((lane == row + 1) & (row < 127) | (lane == row + 127) & (row > 0), 1.0, 0.0))
    shift[0:128] = move
    shift[128:256] = move
    source = row % (2 * per)
    for q in range(per):
        hit = (source == 2 * q) & (lane == 0) | (source == 2 * q + 1) & (lane == 255)
        spot = bf16(jnp.where(hit & (row < 2 * per * vectors), 1.0, 0.0))
        spots[q, 0:128] = spot
        spots[q, 128:256] = spot
    one = jnp.ones((1, 128), F32)
    lane = lanes((height, 128))
    for l in range(levels):
        coefs[0, l] = bf16(jnp.concatenate([one, sten[1, l].astype(F32)[:-1]], axis=0))
        coefs[1, l] = bf16(jnp.concatenate([sten[2, l].astype(F32)[1:], one], axis=0))
        right = jnp.dot(sten[3, l], move[:, 0:128], preferred_element_type=F32)
        left = jnp.dot(sten[4, l], move[:, 128:256], preferred_element_type=F32)
        coefs[2, l] = bf16(jnp.where(lane == 0, 1.0, right))
        coefs[3, l] = bf16(jnp.where(lane == 127, 1.0, left))
    copy.wait()


def final_kernel(
    dims, part, kry, adj, sten, coefs, shift, spots, cw, fwd, back, cols, mine, other,
    out_hbm, comb, low, edges, moved, out, sem,
):
    vectors, levels, fields, height = dims
    half = vectors // 2
    per = levels * fields
    total = jnp.broadcast_to(jnp.sum(part[...], axis=1, keepdims=True), (8, 128))
    mix = [jnp.broadcast_to(total[j : j + 1], (8, 128)) for j in range(vectors)]
    is_low = lax.axis_index("lev") & 1 == 0
    mine_mix = [jnp.where(is_low, mix[k], mix[half + k]) for k in range(half)]
    other_mix = [jnp.where(is_low, mix[half + k], mix[k]) for k in range(half)]

    def times(m, x):
        return (x.reshape(-1, 8, 128) * m).reshape(x.shape)

    rim_f = sum(times(mix[k], fwd[k * 16 : (k + 1) * 16]) for k in range(vectors))
    rim_b = sum(times(mix[k], back[k * 16 : (k + 1) * 16]) for k in range(vectors))
    for q in range(per):
        comb[q, 7:8] = rim_f[q : q + 1]
        comb[q, 8 + height : 9 + height] = rim_b[q : q + 1]

    lane = lanes((8, 128)) // (2 * per)
    weight = jnp.zeros((8, 128), F32)
    for k in range(vectors):
        weight = jnp.where(lane == k, mix[k], weight)
    step = 64
    for i in range(height // step):
        edges[i * step : (i + 1) * step] = split(times(weight, cols[i * step : (i + 1) * step]))

    def combine(l, f):
        for i in range(height // step):
            at = slice(i * step, (i + 1) * step)
            comb[l * fields + f, 8 + i * step : 8 + (i + 1) * step] = sum(
                times(mix[k], kry[k, l, f, at].astype(F32)) for k in range(vectors)
            )

    def column(c):
        for i in range(height // step):
            at = slice(i * step, (i + 1) * step)
            x = 0.0
            for k in range(half):
                here = slice((k * 2 + c) * height + i * step, (k * 2 + c) * height + (i + 1) * step)
                x = x + (times(mine_mix[k], mine[here]) + times(other_mix[k], other[here]))
            for l in reversed(range(levels)):
                q = l * fields + (0 if c == 0 else 3)
                x = x + comb[q, 8 + i * step : 8 + (i + 1) * step]
                low[c, l, at] = cw[c, l, at] * x

    def move(l, f):
        q = l * fields + f
        x = comb[q, 8 : 8 + height]
        moved[q % 2] = jnp.dot(split(x), shift[...], preferred_element_type=F32) + jnp.dot(
            edges[...], spots[q], preferred_element_type=F32
        )

    def stencil(l, f):
        q = l * fields + f
        for i in range(height // step):
            at = slice(i * step, (i + 1) * step)
            first = 8 + i * step
            image = (
                sten[0, l, at].astype(F32) * comb[q, first : first + step]
                + coefs[0, l, at].astype(F32) * comb[q, first - 1 : first + step - 1]
                + coefs[1, l, at].astype(F32) * comb[q, first + 1 : first + step + 1]
                + coefs[2, l, at].astype(F32) * moved[q % 2, at, 0:128]
                + coefs[3, l, at].astype(F32) * moved[q % 2, at, 128:256]
            )
            if f in (1, 4):
                image = image + low[0 if f == 1 else 1, l, at]
            out[l, f, at] = adj[l, f, at] + image

    order = [0, 3] + [f for f in range(fields) if f not in (0, 3)]
    planes = [(l, f) for f in order for l in range(levels)]
    combine(*planes[0])
    copies = []
    for n, (l, f) in enumerate(planes):
        if n + 1 < len(planes):
            combine(*planes[n + 1])
        if n == 2 * levels - 1:
            column(0)
            column(1)
        move(l, f)
        stencil(l, f)
        copy = pltpu.make_async_copy(out.at[l, f], out_hbm.at[l, f], sem.at[n])
        copy.start()
        copies.append(copy)
    for copy in copies:
        copy.wait()


def final_scratch(dims):
    _, levels, fields, height = dims
    return [
        pltpu.VMEM((levels * fields, height + 16, 128), F32),
        pltpu.VMEM((2, levels, height, 128), F32),
        pltpu.VMEM((height, 256), jnp.bfloat16),
        pltpu.VMEM((2, height, 256), F32),
        pltpu.VMEM((levels, fields, height, 128), F32),
        pltpu.SemaphoreType.DMA((levels * fields,)),
    ]


def pair_kernel(pack, got, o):
    o[...] = pack[-8:] + got[-8:]


def segment_kernel(got, mine, token, held, o):
    del token, held
    o[...] = mine[...] + got[0 : o.shape[0]]


def join_kernel(a, b, near, held, o):
    del near, held
    o[0:8] = a[...] + b[...]


def add_kernel(a, b, *rest):
    o = rest[-1]
    o[...] = a[0:8] + b[0:8]


def keep_kernel(x, token, held, o):
    del token, held
    o[...] = x[...]


def after(x, token, held):
    return local(
        keep_kernel,
        "after",
        12,
        pltpu.VMEM(x.shape, F32),
        [IN_VMEM] * 3,
        *map(pinned, (x, token, held)),
    )


def below_kernel(group_bits, got, mine, token, held, *refs):
    del token, held
    above, (send_o, mine_o) = refs[:-2], refs[-2:]
    group = lax.axis_index("lev")
    upper = group & 1 == 1
    split = mine.shape[0]
    step = 256

    def body(i, carry):
        at = pl.ds(pl.multiple_of(i * step, step), step)
        x = jnp.zeros((step, 128), F32)
        for bit, ref in zip(group_bits, above, strict=True):
            x = x + jnp.where(group & bit == 0, ref[at], 0.0)
        send_o[at] = x + jnp.where(upper, mine[at], 0.0)
        mine_o[at] = x + jnp.where(upper, 0.0, got[at])
        return carry

    lax.fori_loop(0, split // step, body, 0)


def local(kernel, name, us, out_shape, in_specs, *args, limit=SMALL, **more):
    return pl.pallas_call(
        kernel,
        out_shape=out_shape,
        in_specs=in_specs,
        out_specs=jax.tree.map(lambda _: IN_VMEM, out_shape),
        compiler_params=pltpu.CompilerParams(vmem_limit_bytes=limit),
        cost_estimate=pl.CostEstimate(
            flops=int(us * 1e9), bytes_accessed=int(us * 3.5e6), transcendentals=0
        ),
        name=name,
        **more,
    )(*args)


def add(a, b, *held):
    return local(
        add_kernel, "add", 12, pltpu.VMEM((8, 128), F32), [IN_VMEM] * (2 + len(held)),
        *map(pinned, (a, b, *held)),
    )


def per_device(krylov, adjoint, projected, stencil, column_weight, seam_turns):
    vectors, levels, fields, height, width = krylov.shape
    dims = (vectors, levels, fields, height)
    half, per = vectors // 2, levels * fields
    tiles, groups = lax.axis_size("tile"), lax.axis_size("lev")
    count = levels * fields * height * width * tiles * groups
    total_rows = vectors * height
    bf = krylov.dtype
    dma = pltpu.SemaphoreType.DMA

    kry, pack, mine, adj = local(
        functools.partial(dots_kernel, dims, count),
        "dots",
        2,
        (
            pltpu.VMEM(krylov.shape, bf),
            pltpu.VMEM((total_rows + 8, width), F32),
            pltpu.VMEM((total_rows, width), F32),
            pltpu.VMEM(adjoint.shape, F32),
        ),
        [IN_HBM] * 3,
        *map(in_hbm, (projected, krylov, adjoint)),
        scratch_shapes=[
            pltpu.VMEM(projected.shape, F32),
            pltpu.VMEM((vectors, 8, 128), F32),
            dma((fields,)),
            dma((fields,)),
            dma,
        ],
    )
    sten, near, far, cols = local(
        functools.partial(strips_kernel, dims),
        "strips",
        1.5,
        (
            pltpu.VMEM(stencil.shape, bf),
            pltpu.VMEM((vectors * 16 + 8, width), F32),
            pltpu.VMEM((vectors * 16, width), F32),
            pltpu.VMEM((2 * vectors * per, height), F32),
        ),
        [IN_VMEM, IN_HBM],
        pinned(kry),
        in_hbm(stencil),
        scratch_shapes=[pltpu.VMEM((height, width), F32), dma],
    )

    first = exchange(pack, "lev", 1)
    part = local(
        pair_kernel, "pair", 0.1, pltpu.VMEM((8, width), F32), [IN_VMEM] * 2, pinned(pack), pinned(first)
    )
    segment = local(
        segment_kernel,
        "segment",
        12,
        pltpu.VMEM(mine.shape, F32),
        [IN_VMEM] * 4,
        *map(pinned, (first, mine, part, kry)),
    )
    above = []
    for bit in bits("lev")[1:]:
        if above:
            segment = segment + above[-1]
        above.append(exchange(segment, "lev", bit))
    cols = after(cols, part, kry)
    up = shifted(cols, "tile", STRIDE)
    down = up if (2 * STRIDE) % tiles == 0 else shifted(cols, "tile", -STRIDE)

    for bit in bits("lev")[1:-1]:
        part = add(part, exchange(part, "lev", bit))
    coefs, shift, spots, cw = local(
        functools.partial(tables_kernel, dims),
        "tables",
        1.5,
        (
            pltpu.VMEM((4,) + stencil.shape[1:], bf),
            pltpu.VMEM((256, 256), bf),
            pltpu.VMEM((per, 256, 256), bf),
            pltpu.VMEM(column_weight.shape, F32),
        ),
        [IN_VMEM, IN_HBM, IN_VMEM],
        pinned(sten),
        in_hbm(column_weight),
        pinned(part),
        scratch_shapes=[dma],
    )
    got = exchange(part, "lev", bits("lev")[-1])
    near = local(
        join_kernel,
        "join",
        12,
        pltpu.VMEM(near.shape, F32),
        [IN_VMEM] * 4,
        *map(pinned, (part, got, near, shift)),
        input_output_aliases={2: 0},
    )
    far = after(far, near, kry)
    got = exchange(near, "tile", 1)
    part = add(near, got)
    near = got
    far = lax.ppermute(
        far, "tile", [(i, (i + 1 if i % 2 else i - 1) % tiles) for i in range(tiles)]
    )
    for bit in bits("tile")[1:-1]:
        part = add(part, exchange(part, "tile", bit))
    token = part
    send, mine = local(
        functools.partial(below_kernel, bits("lev")[1:]),
        "below",
        12,
        (pltpu.VMEM(mine.shape, F32), pltpu.VMEM(mine.shape, F32)),
        [IN_VMEM] * (4 + len(above)),
        *map(pinned, (first, mine, token, kry, *above)),
    )
    other = exchange(send, "lev", 1)

    fwd, back, cols = local(
        functools.partial(turn_kernel, dims),
        "turn",
        1,
        (
            pltpu.VMEM(far.shape, F32),
            pltpu.VMEM(far.shape, F32),
            pltpu.VMEM((height, width), F32),
        ),
        [IN_VMEM] * 5,
        *map(pinned, (seam_turns, near, far, up, down)),
    )

    for bit in bits("tile")[-1:]:
        part = add(part, exchange(part, "tile", bit))

    return pl.pallas_call(
        functools.partial(final_kernel, dims),
        out_shape=jax.ShapeDtypeStruct(adjoint.shape, F32),
        in_specs=[IN_VMEM] * 13,
        out_specs=IN_HBM,
        scratch_shapes=final_scratch(dims),
        compiler_params=pltpu.CompilerParams(vmem_limit_bytes=LARGE),
        name="final",
    )(
        *map(
            pinned,
            (part, kry, adj, sten, coefs, shift, spots, cw, fwd, back, cols, mine, other),
        )
    )


def solution(mesh):
    placed = (
        P(None, "lev", None, "tile", None),
        P("lev", None, "tile", None),
        P(),
        P(None, "lev", "tile", None),
        P(None, "lev", "tile", None),
        P("tile", None),
    )
    return jax.shard_map(
        per_device,
        mesh=mesh,
        in_specs=placed,
        out_specs=P("lev", None, "tile", None),
        check_vma=False,
    )
```

```python
import functools

import jax
import jax.numpy as jnp
from jax import lax
from jax.experimental import pallas as pl
from jax.experimental.pallas import tpu as pltpu
from jax.sharding import PartitionSpec as P

STRIDE = 4
F32 = jnp.float32
SMALL = 4 * 1024 * 1024
LARGE = 8 * 1024 * 1024

IN_HBM = pl.BlockSpec(memory_space=pltpu.HBM)
IN_VMEM = pl.BlockSpec(memory_space=pltpu.VMEM)


def pinned(x):
    return pltpu.with_memory_space_constraint(x, pltpu.VMEM)


def in_hbm(x):
    return pltpu.with_memory_space_constraint(x, pltpu.HBM)


def exchange(x, axis, bit):
    size = lax.axis_size(axis)
    return lax.ppermute(x, axis, [(i, i ^ bit) for i in range(size)])


def shifted(x, axis, steps):
    size = lax.axis_size(axis)
    return lax.ppermute(x, axis, [(i, (i + steps) % size) for i in range(size)])


def bits(axis):
    size = lax.axis_size(axis)
    return [1 << b for b in range(size.bit_length() - 1)]


def lanes(shape):
    return lax.broadcasted_iota(jnp.int32, shape, len(shape) - 1)


def rows(shape):
    return lax.broadcasted_iota(jnp.int32, shape, len(shape) - 2)


def bf16(x):
    return x.astype(jnp.bfloat16)


def split(x):
    high = bf16(x)
    return jnp.concatenate([high, bf16(x - high.astype(F32))], axis=1)


def ends_to(last, first):
    row, lane = rows((16, 128)), lanes((16, 128))
    top = bf16(jnp.where((row == 0) & first(lane), 1.0, 0.0))
    bottom = bf16(jnp.where((row == 15) & last(lane), 1.0, 0.0))
    return jnp.concatenate([top, jnp.zeros((96, 128), jnp.bfloat16), bottom], axis=0)


def dots_kernel(
    dims, count, projected, kry, adj, kry_v, pack, mine, adj_v, proj_v, mixer, sem_k, sem_a, sem_p
):
    vectors, levels, fields, height = dims
    half = vectors // 2
    upper = lax.axis_index("lev") & 1 == 1
    order = [0, 3] + [f for f in range(fields) if f not in (0, 3)]
    copy_p = pltpu.make_async_copy(projected, proj_v, sem_p)
    copy_p.start()
    copies = {}
    for f in order:
        copies[f] = (
            pltpu.make_async_copy(kry.at[:, :, f], kry_v.at[:, :, f], sem_k.at[f]),
            pltpu.make_async_copy(adj.at[:, f], adj_v.at[:, f], sem_a.at[f]),
        )
        for copy in copies[f]:
            copy.start()
    step = 128
    accs = [jnp.zeros((8, 128), F32) for _ in range(vectors)]
    for f in order:
        for copy in copies[f]:
            copy.wait()
        for l in range(levels):

            def body(i, accs, f=f, l=l):
                start = pl.multiple_of(i * step, step)
                at = pl.ds(start, step)
                y = adj_v[l, f, at]
                xs = [kry_v[k, l, f, at].astype(F32) for k in range(vectors)]
                if f in (0, 3):
                    for k in range(half):
                        to = pl.ds(start + (k * 2 + (0 if f == 0 else 1)) * height, step)
                        a, b = xs[k], xs[half + k]
                        for ref, x in ((mine, jnp.where(upper, b, a)), (pack, jnp.where(upper, a, b))):
                            ref[to] = x if l == 0 else ref[to] + x
                out = [
                    acc + jnp.sum((x * y).reshape(step // 8, 8, 128), axis=0)
                    for acc, x in zip(accs, xs, strict=True)
                ]
                return out

            accs = lax.fori_loop(0, height // step, body, accs)
    copy_p.wait()
    r = rows((8, 128))
    for k in range(vectors):
        m = jnp.zeros((8, 128), F32)
        for j in range(vectors):
            m = jnp.where(r == j, proj_v[k : k + 1, j : j + 1] * (0.5 / count), m)
        mixer[k] = m
    total = jnp.zeros((8, 128), F32)
    for k in range(vectors):
        total = total + mixer[k] * jnp.sum(accs[k], axis=0, keepdims=True)
    pack[vectors * height : vectors * height + 8] = total


def strips_kernel(dims, kry_v, sten, sten_v, near, far, cols_t, cols, sem):
    vectors, levels, fields, height = dims
    per = levels * fields
    even_tile = lax.axis_index("tile") & 1 == 0
    copy = pltpu.make_async_copy(sten, sten_v, sem)
    copy.start()
    near[...] = jnp.zeros_like(near)
    far[...] = jnp.zeros_like(far)
    planes = [(k, l, f) for k in range(vectors) for l in range(levels) for f in range(fields)]
    cols[...] = jnp.dot(
        jnp.concatenate([kry_v[p] for p in planes], axis=1),
        jnp.concatenate(
            [
                ends_to(lambda lane, s=2 * s: lane == s, lambda lane, s=2 * s: lane == s + 1)
                for s in range(len(planes))
            ],
            axis=0,
        ),
        preferred_element_type=F32,
    )
    copy.wait()
    tail = height - 16
    for l in range(levels):
        last = sten_v[1, l, tail:height].astype(F32)
        first = sten_v[2, l, 0:16].astype(F32)
        for k in range(vectors):
            for f in range(fields):
                s = k * 16 + l * fields + f
                fwd = (kry_v[k, l, f, tail:height].astype(F32) * last)[15:16]
                back = (kry_v[k, l, f, 0:16].astype(F32) * first)[0:1]
                near[8 + s : 9 + s] = jnp.where(even_tile, fwd, back)
                far[s : s + 1] = jnp.where(even_tile, back, fwd)
    none = lambda lane: lane < 0
    weights = []
    for l in range(levels):
        here = lambda lane, l=l: lane % (2 * per) // (2 * fields) == l
        weights.append(ends_to(lambda lane, here=here: here(lane) & (lane % 2 == 0), none))
        weights.append(ends_to(none, lambda lane, here=here: here(lane) & (lane % 2 == 1)))
    coeff = jnp.dot(
        jnp.concatenate([sten_v[d, l] for l in range(levels) for d in (3, 4)], axis=1),
        jnp.concatenate(weights, axis=0),
        preferred_element_type=F32,
    )
    cols_t[...] = jnp.transpose(cols[...] * coeff)[0 : cols_t.shape[0]]


def turn_of(r):
    cosine = jnp.where(r == 0, 1.0, jnp.where(r == 2, -1.0, 0.0)).astype(F32)
    sine = jnp.where(r == 1, 1.0, jnp.where(r == 3, -1.0, 0.0)).astype(F32)
    return cosine, sine


def turn_kernel(dims, turns, near, far, up, down, fwd_o, back_o, cols_o):
    vectors, levels, fields, height = dims
    per = levels * fields
    n = vectors * 16
    flip = bf16(jnp.where(lanes((128, 128)) + rows((128, 128)) == 127, 1.0, 0.0))
    flip = jnp.concatenate([flip, flip], axis=0)
    r = rows((n, 128)) % 16
    field = r % fields
    real = r < per
    even_tile = lax.axis_index("tile") & 1 == 0
    for side, out in ((0, fwd_o), (1, back_o)):
        turning = jnp.broadcast_to(turns[0:1, side : side + 1], (n, 128))
        first, second = (far[...], near[8:]) if side == 0 else (near[8:], far[...])
        x = jnp.where(even_tile, first, second)
        x = jnp.where(
            turning % 2 == 1,
            jnp.dot(split(x), flip, preferred_element_type=F32),
            x,
        )
        cosine, sine = turn_of(turning)
        u = cosine * x - sine * pltpu.roll(x, n - 1, 0)
        v = sine * pltpu.roll(x, 1, 0) + cosine * x
        out[...] = jnp.where(real & (field == 2), u, jnp.where(real & (field == 3), v, x))
    strips = up.shape[0]
    r = rows((strips, 1))
    even = r % 2 == 0
    x = jnp.where(even, up[...], down[...])
    mirror = bf16(jnp.where(lanes((height, height)) + rows((height, height)) == height - 1, 1.0, 0.0))
    mirrored = jnp.dot(
        split(x), jnp.concatenate([mirror, mirror], axis=0), preferred_element_type=F32
    )
    turning = jnp.where(even, turns[0:1, 2:3], turns[0:1, 3:4])
    x = jnp.where(turning % 2 == 1, mirrored, x)
    cosine, sine = turn_of(turning)
    field = r % (2 * fields) // 2
    u = cosine * x - sine * pltpu.roll(x, strips - 2, 0)
    v = sine * pltpu.roll(x, 2, 0) + cosine * x
    x = jnp.where(field == 2, u, jnp.where(field == 3, v, x))
    cols_o[...] = jnp.transpose(
        jnp.concatenate([x, jnp.zeros((128 - strips, height), F32)], axis=0)
    )


def tables_kernel(dims, sten, cw, token, coefs, shift, spots, cw_v, sem):
    del token
    vectors, levels, fields, height = dims
    per = levels * fields
    copy = pltpu.make_async_copy(cw, cw_v, sem)
    copy.start()
    row, lane = rows((128, 256)), lanes((128, 256))
    move = bf16(jnp.where((lane == row + 1) & (row < 127) | (lane == row + 127) & (row > 0), 1.0, 0.0))
    shift[0:128] = move
    shift[128:256] = move
    source = row % (2 * per)
    for q in range(per):
        hit = (source == 2 * q) & (lane == 0) | (source == 2 * q + 1) & (lane == 255)
        spot = bf16(jnp.where(hit & (row < 2 * per * vectors), 1.0, 0.0))
        spots[q, 0:128] = spot
        spots[q, 128:256] = spot
    one = jnp.ones((1, 128), F32)
    lane = lanes((height, 128))
    for l in range(levels):
        coefs[0, l] = bf16(jnp.concatenate([one, sten[1, l].astype(F32)[:-1]], axis=0))
        coefs[1, l] = bf16(jnp.concatenate([sten[2, l].astype(F32)[1:], one], axis=0))
        right = jnp.dot(sten[3, l], move[:, 0:128], preferred_element_type=F32)
        left = jnp.dot(sten[4, l], move[:, 128:256], preferred_element_type=F32)
        coefs[2, l] = bf16(jnp.where(lane == 0, 1.0, right))
        coefs[3, l] = bf16(jnp.where(lane == 127, 1.0, left))
    copy.wait()


def final_kernel(
    dims, part, kry, adj, sten, coefs, shift, spots, cw, fwd, back, cols, mine, other,
    out_hbm, comb, low, edges, moved, out, sem,
):
    vectors, levels, fields, height = dims
    half = vectors // 2
    per = levels * fields
    total = jnp.broadcast_to(jnp.sum(part[...], axis=1, keepdims=True), (8, 128))
    mix = [jnp.broadcast_to(total[j : j + 1], (8, 128)) for j in range(vectors)]
    is_low = lax.axis_index("lev") & 1 == 0
    mine_mix = [jnp.where(is_low, mix[k], mix[half + k]) for k in range(half)]
    other_mix = [jnp.where(is_low, mix[half + k], mix[k]) for k in range(half)]

    def times(m, x):
        return (x.reshape(-1, 8, 128) * m).reshape(x.shape)

    rim_f = sum(times(mix[k], fwd[k * 16 : (k + 1) * 16]) for k in range(vectors))
    rim_b = sum(times(mix[k], back[k * 16 : (k + 1) * 16]) for k in range(vectors))
    for q in range(per):
        comb[q, 7:8] = rim_f[q : q + 1]
        comb[q, 8 + height : 9 + height] = rim_b[q : q + 1]

    lane = lanes((8, 128)) // (2 * per)
    weight = jnp.zeros((8, 128), F32)
    for k in range(vectors):
        weight = jnp.where(lane == k, mix[k], weight)
    step = 64
    for i in range(height // step):
        edges[i * step : (i + 1) * step] = split(times(weight, cols[i * step : (i + 1) * step]))

    def combine(l, f):
        for i in range(height // step):
            at = slice(i * step, (i + 1) * step)
            comb[l * fields + f, 8 + i * step : 8 + (i + 1) * step] = sum(
                times(mix[k], kry[k, l, f, at].astype(F32)) for k in range(vectors)
            )

    def column(l):
        for c, f in ((0, 0), (1, 3)):
            for i in range(height // step):
                at = slice(i * step, (i + 1) * step)
                if l == levels - 1:
                    x = 0.0
                    for k in range(half):
                        start = (k * 2 + c) * height + i * step
                        x = x + (
                            times(mine_mix[k], mine[start : start + step])
                            + times(other_mix[k], other[start : start + step])
                        )
                else:
                    x = low[c, at]
                low[c, at] = x + comb[l * fields + f, 8 + i * step : 8 + (i + 1) * step]

    def move(l, f):
        q = l * fields + f
        x = comb[q, 8 : 8 + height]
        moved[f] = jnp.dot(split(x), shift[...], preferred_element_type=F32) + jnp.dot(
            edges[...], spots[q], preferred_element_type=F32
        )

    copies = []

    def stencil(l):
        size, block = 32, 64
        for i in range(height // size):
            at = slice(i * size, (i + 1) * size)
            first = 8 + i * size
            c0 = sten[0, l, at].astype(F32)
            c1, c2, c3, c4 = (coefs[d, l, at].astype(F32) for d in range(4))
            for f in range(fields):
                q = l * fields + f
                image = (
                    c0 * comb[q, first : first + size]
                    + c1 * comb[q, first - 1 : first + size - 1]
                    + c2 * comb[q, first + 1 : first + size + 1]
                    + c3 * moved[f, at, 0:128]
                    + c4 * moved[f, at, 128:256]
                )
                if f in (1, 4):
                    c = 0 if f == 1 else 1
                    image = image + cw[c, l, at] * low[c, at]
                out[l, f, at] = adj[l, f, at] + image
            if (i + 1) * size % block == 0:
                n = (i + 1) * size // block - 1
                at = slice(n * block, (n + 1) * block)
                copy = pltpu.make_async_copy(
                    out.at[l, :, at], out_hbm.at[l, :, at], sem.at[len(copies)]
                )
                copy.start()
                copies.append(copy)

    for l in reversed(range(levels)):
        for f in range(fields):
            combine(l, f)
        column(l)
        for f in range(fields):
            move(l, f)
        stencil(l)
    for copy in copies:
        copy.wait()


def final_scratch(dims):
    _, levels, fields, height = dims
    return [
        pltpu.VMEM((levels * fields, height + 16, 128), F32),
        pltpu.VMEM((2, height, 128), F32),
        pltpu.VMEM((height, 256), jnp.bfloat16),
        pltpu.VMEM((fields, height, 256), F32),
        pltpu.VMEM((levels, fields, height, 128), F32),
        pltpu.SemaphoreType.DMA((levels * height // 64,)),
    ]


def pair_kernel(pack, got, o):
    o[...] = pack[-8:] + got[-8:]


def segment_kernel(got, mine, token, held, o):
    del token, held
    o[...] = mine[...] + got[0 : o.shape[0]]


def join_kernel(a, b, near, held, o):
    del near, held
    o[0:8] = a[...] + b[...]


def add_kernel(a, b, *rest):
    o = rest[-1]
    o[...] = a[0:8] + b[0:8]


def keep_kernel(x, token, held, o):
    del token, held
    o[...] = x[...]


def after(x, token, held):
    return local(
        keep_kernel,
        "after",
        12,
        pltpu.VMEM(x.shape, F32),
        [IN_VMEM] * 3,
        *map(pinned, (x, token, held)),
    )


def below_kernel(group_bits, got, mine, token, held, *refs):
    del token, held
    above, (send_o, mine_o) = refs[:-2], refs[-2:]
    group = lax.axis_index("lev")
    upper = group & 1 == 1
    split = mine.shape[0]
    step = 256

    def body(i, carry):
        at = pl.ds(pl.multiple_of(i * step, step), step)
        x = jnp.zeros((step, 128), F32)
        for bit, ref in zip(group_bits, above, strict=True):
            x = x + jnp.where(group & bit == 0, ref[at], 0.0)
        send_o[at] = x + jnp.where(upper, mine[at], 0.0)
        mine_o[at] = x + jnp.where(upper, 0.0, got[at])
        return carry

    lax.fori_loop(0, split // step, body, 0)


def local(kernel, name, us, out_shape, in_specs, *args, limit=SMALL, **more):
    return pl.pallas_call(
        kernel,
        out_shape=out_shape,
        in_specs=in_specs,
        out_specs=jax.tree.map(lambda _: IN_VMEM, out_shape),
        compiler_params=pltpu.CompilerParams(vmem_limit_bytes=limit),
        cost_estimate=pl.CostEstimate(
            flops=int(us * 1e9), bytes_accessed=int(us * 3.5e6), transcendentals=0
        ),
        name=name,
        **more,
    )(*args)


def add(a, b, *held):
    return local(
        add_kernel, "add", 12, pltpu.VMEM((8, 128), F32), [IN_VMEM] * (2 + len(held)),
        *map(pinned, (a, b, *held)),
    )


def per_device(krylov, adjoint, projected, stencil, column_weight, seam_turns):
    vectors, levels, fields, height, width = krylov.shape
    dims = (vectors, levels, fields, height)
    half, per = vectors // 2, levels * fields
    tiles, groups = lax.axis_size("tile"), lax.axis_size("lev")
    count = levels * fields * height * width * tiles * groups
    total_rows = vectors * height
    bf = krylov.dtype
    dma = pltpu.SemaphoreType.DMA

    kry, pack, mine, adj = local(
        functools.partial(dots_kernel, dims, count),
        "dots",
        2,
        (
            pltpu.VMEM(krylov.shape, bf),
            pltpu.VMEM((total_rows + 8, width), F32),
            pltpu.VMEM((total_rows, width), F32),
            pltpu.VMEM(adjoint.shape, F32),
        ),
        [IN_HBM] * 3,
        *map(in_hbm, (projected, krylov, adjoint)),
        scratch_shapes=[
            pltpu.VMEM(projected.shape, F32),
            pltpu.VMEM((vectors, 8, 128), F32),
            dma((fields,)),
            dma((fields,)),
            dma,
        ],
    )
    sten, near, far, cols = local(
        functools.partial(strips_kernel, dims),
        "strips",
        1.5,
        (
            pltpu.VMEM(stencil.shape, bf),
            pltpu.VMEM((vectors * 16 + 8, width), F32),
            pltpu.VMEM((vectors * 16, width), F32),
            pltpu.VMEM((2 * vectors * per, height), F32),
        ),
        [IN_VMEM, IN_HBM],
        pinned(kry),
        in_hbm(stencil),
        scratch_shapes=[pltpu.VMEM((height, width), F32), dma],
    )

    first = exchange(pack, "lev", 1)
    part = local(
        pair_kernel, "pair", 0.1, pltpu.VMEM((8, width), F32), [IN_VMEM] * 2, pinned(pack), pinned(first)
    )
    segment = local(
        segment_kernel,
        "segment",
        12,
        pltpu.VMEM(mine.shape, F32),
        [IN_VMEM] * 4,
        *map(pinned, (first, mine, part, kry)),
    )
    above = []
    for bit in bits("lev")[1:]:
        if above:
            segment = segment + above[-1]
        above.append(exchange(segment, "lev", bit))
    cols = after(cols, part, kry)
    up = shifted(cols, "tile", STRIDE)
    down = up if (2 * STRIDE) % tiles == 0 else shifted(cols, "tile", -STRIDE)

    for bit in bits("lev")[1:-1]:
        part = add(part, exchange(part, "lev", bit))
    coefs, shift, spots, cw = local(
        functools.partial(tables_kernel, dims),
        "tables",
        1.5,
        (
            pltpu.VMEM((4,) + stencil.shape[1:], bf),
            pltpu.VMEM((256, 256), bf),
            pltpu.VMEM((per, 256, 256), bf),
            pltpu.VMEM(column_weight.shape, F32),
        ),
        [IN_VMEM, IN_HBM, IN_VMEM],
        pinned(sten),
        in_hbm(column_weight),
        pinned(part),
        scratch_shapes=[dma],
    )
    got = exchange(part, "lev", bits("lev")[-1])
    near = local(
        join_kernel,
        "join",
        12,
        pltpu.VMEM(near.shape, F32),
        [IN_VMEM] * 4,
        *map(pinned, (part, got, near, shift)),
        input_output_aliases={2: 0},
    )
    far = after(far, near, kry)
    got = exchange(near, "tile", 1)
    part = add(near, got)
    near = got
    far = lax.ppermute(
        far, "tile", [(i, (i + 1 if i % 2 else i - 1) % tiles) for i in range(tiles)]
    )
    for bit in bits("tile")[1:-1]:
        part = add(part, exchange(part, "tile", bit))
    token = part
    send, mine = local(
        functools.partial(below_kernel, bits("lev")[1:]),
        "below",
        12,
        (pltpu.VMEM(mine.shape, F32), pltpu.VMEM(mine.shape, F32)),
        [IN_VMEM] * (4 + len(above)),
        *map(pinned, (first, mine, token, kry, *above)),
    )
    other = exchange(send, "lev", 1)

    fwd, back, cols = local(
        functools.partial(turn_kernel, dims),
        "turn",
        1,
        (
            pltpu.VMEM(far.shape, F32),
            pltpu.VMEM(far.shape, F32),
            pltpu.VMEM((height, width), F32),
        ),
        [IN_VMEM] * 5,
        *map(pinned, (seam_turns, near, far, up, down)),
    )

    for bit in bits("tile")[-1:]:
        part = add(part, exchange(part, "tile", bit))

    return pl.pallas_call(
        functools.partial(final_kernel, dims),
        out_shape=jax.ShapeDtypeStruct(adjoint.shape, F32),
        in_specs=[IN_VMEM] * 13,
        out_specs=IN_HBM,
        scratch_shapes=final_scratch(dims),
        compiler_params=pltpu.CompilerParams(vmem_limit_bytes=LARGE),
        name="final",
    )(
        *map(
            pinned,
            (part, kry, adj, sten, coefs, shift, spots, cw, fwd, back, cols, mine, other),
        )
    )


def solution(mesh):
    placed = (
        P(None, "lev", None, "tile", None),
        P("lev", None, "tile", None),
        P(),
        P(None, "lev", "tile", None),
        P(None, "lev", "tile", None),
        P("tile", None),
    )
    return jax.shard_map(
        per_device,
        mesh=mesh,
        in_specs=placed,
        out_specs=P("lev", None, "tile", None),
        check_vma=False,
    )
```

```python
import functools

import jax
import jax.numpy as jnp
from jax import lax
from jax.experimental import pallas as pl
from jax.experimental.pallas import tpu as pltpu
from jax.sharding import PartitionSpec as P

STRIDE = 4
F32 = jnp.float32
SMALL = 4 * 1024 * 1024
LARGE = 8 * 1024 * 1024

IN_HBM = pl.BlockSpec(memory_space=pltpu.HBM)
IN_VMEM = pl.BlockSpec(memory_space=pltpu.VMEM)


def pinned(x):
    return pltpu.with_memory_space_constraint(x, pltpu.VMEM)


def in_hbm(x):
    return pltpu.with_memory_space_constraint(x, pltpu.HBM)


def exchange(x, axis, bit):
    size = lax.axis_size(axis)
    return lax.ppermute(x, axis, [(i, i ^ bit) for i in range(size)])


def shifted(x, axis, steps):
    size = lax.axis_size(axis)
    return lax.ppermute(x, axis, [(i, (i + steps) % size) for i in range(size)])


def bits(axis):
    size = lax.axis_size(axis)
    return [1 << b for b in range(size.bit_length() - 1)]


def lanes(shape):
    return lax.broadcasted_iota(jnp.int32, shape, len(shape) - 1)


def rows(shape):
    return lax.broadcasted_iota(jnp.int32, shape, len(shape) - 2)


def bf16(x):
    return x.astype(jnp.bfloat16)


def split(x):
    high = bf16(x)
    return jnp.concatenate([high, bf16(x - high.astype(F32))], axis=1)


def ends_to(last, first):
    row, lane = rows((16, 128)), lanes((16, 128))
    top = bf16(jnp.where((row == 0) & first(lane), 1.0, 0.0))
    bottom = bf16(jnp.where((row == 15) & last(lane), 1.0, 0.0))
    return jnp.concatenate([top, jnp.zeros((96, 128), jnp.bfloat16), bottom], axis=0)


def dots_kernel(
    dims, count, projected, kry, adj, kry_v, pack, mine, adj_v, proj_v, mixer, sem_k, sem_a, sem_p
):
    vectors, levels, fields, height = dims
    half = vectors // 2
    upper = lax.axis_index("lev") & 1 == 1
    order = [0, 3] + [f for f in range(fields) if f not in (0, 3)]
    copy_p = pltpu.make_async_copy(projected, proj_v, sem_p)
    copy_p.start()
    copies = {}
    for f in order:
        copies[f] = (
            pltpu.make_async_copy(kry.at[:, :, f], kry_v.at[:, :, f], sem_k.at[f]),
            pltpu.make_async_copy(adj.at[:, f], adj_v.at[:, f], sem_a.at[f]),
        )
        for copy in copies[f]:
            copy.start()
    step = 128
    accs = [jnp.zeros((8, 128), F32) for _ in range(vectors)]
    for f in order:
        for copy in copies[f]:
            copy.wait()
        for l in range(levels):

            def body(i, accs, f=f, l=l):
                start = pl.multiple_of(i * step, step)
                at = pl.ds(start, step)
                y = adj_v[l, f, at]
                xs = [kry_v[k, l, f, at].astype(F32) for k in range(vectors)]
                if f in (0, 3):
                    for k in range(half):
                        to = pl.ds(start + (k * 2 + (0 if f == 0 else 1)) * height, step)
                        a, b = xs[k], xs[half + k]
                        for ref, x in ((mine, jnp.where(upper, b, a)), (pack, jnp.where(upper, a, b))):
                            ref[to] = x if l == 0 else ref[to] + x
                out = [
                    acc + jnp.sum((x * y).reshape(step // 8, 8, 128), axis=0)
                    for acc, x in zip(accs, xs, strict=True)
                ]
                return out

            accs = lax.fori_loop(0, height // step, body, accs)
    copy_p.wait()
    r = rows((8, 128))
    for k in range(vectors):
        m = jnp.zeros((8, 128), F32)
        for j in range(vectors):
            m = jnp.where(r == j, proj_v[k : k + 1, j : j + 1] * (0.5 / count), m)
        mixer[k] = m
    total = jnp.zeros((8, 128), F32)
    for k in range(vectors):
        total = total + mixer[k] * jnp.sum(accs[k], axis=0, keepdims=True)
    pack[vectors * height : vectors * height + 8] = total


def strips_kernel(dims, kry_v, sten, sten_v, near, far, cols_t, cols, sem):
    vectors, levels, fields, height = dims
    per = levels * fields
    even_tile = lax.axis_index("tile") & 1 == 0
    copy = pltpu.make_async_copy(sten, sten_v, sem)
    copy.start()
    near[...] = jnp.zeros_like(near)
    far[...] = jnp.zeros_like(far)
    planes = [(k, l, f) for k in range(vectors) for l in range(levels) for f in range(fields)]
    cols[...] = jnp.dot(
        jnp.concatenate([kry_v[p] for p in planes], axis=1),
        jnp.concatenate(
            [
                ends_to(lambda lane, s=2 * s: lane == s, lambda lane, s=2 * s: lane == s + 1)
                for s in range(len(planes))
            ],
            axis=0,
        ),
        preferred_element_type=F32,
    )
    copy.wait()
    tail = height - 16
    for l in range(levels):
        last = sten_v[1, l, tail:height].astype(F32)
        first = sten_v[2, l, 0:16].astype(F32)
        for k in range(vectors):
            for f in range(fields):
                s = k * 16 + l * fields + f
                fwd = (kry_v[k, l, f, tail:height].astype(F32) * last)[15:16]
                back = (kry_v[k, l, f, 0:16].astype(F32) * first)[0:1]
                near[8 + s : 9 + s] = jnp.where(even_tile, fwd, back)
                far[s : s + 1] = jnp.where(even_tile, back, fwd)
    none = lambda lane: lane < 0
    weights = []
    for l in range(levels):
        here = lambda lane, l=l: lane % (2 * per) // (2 * fields) == l
        weights.append(ends_to(lambda lane, here=here: here(lane) & (lane % 2 == 0), none))
        weights.append(ends_to(none, lambda lane, here=here: here(lane) & (lane % 2 == 1)))
    coeff = jnp.dot(
        jnp.concatenate([sten_v[d, l] for l in range(levels) for d in (3, 4)], axis=1),
        jnp.concatenate(weights, axis=0),
        preferred_element_type=F32,
    )
    cols_t[...] = jnp.transpose(cols[...] * coeff)[0 : cols_t.shape[0]]


def turn_of(r):
    cosine = jnp.where(r == 0, 1.0, jnp.where(r == 2, -1.0, 0.0)).astype(F32)
    sine = jnp.where(r == 1, 1.0, jnp.where(r == 3, -1.0, 0.0)).astype(F32)
    return cosine, sine


def turn_kernel(dims, turns, near, far, up, down, fwd_o, back_o, cols_o):
    vectors, levels, fields, height = dims
    per = levels * fields
    n = vectors * 16
    flip = bf16(jnp.where(lanes((128, 128)) + rows((128, 128)) == 127, 1.0, 0.0))
    flip = jnp.concatenate([flip, flip], axis=0)
    r = rows((n, 128)) % 16
    field = r % fields
    real = r < per
    even_tile = lax.axis_index("tile") & 1 == 0
    for side, out in ((0, fwd_o), (1, back_o)):
        turning = jnp.broadcast_to(turns[0:1, side : side + 1], (n, 128))
        first, second = (far[...], near[8:]) if side == 0 else (near[8:], far[...])
        x = jnp.where(even_tile, first, second)
        x = jnp.where(
            turning % 2 == 1,
            jnp.dot(split(x), flip, preferred_element_type=F32),
            x,
        )
        cosine, sine = turn_of(turning)
        u = cosine * x - sine * pltpu.roll(x, n - 1, 0)
        v = sine * pltpu.roll(x, 1, 0) + cosine * x
        out[...] = jnp.where(real & (field == 2), u, jnp.where(real & (field == 3), v, x))
    strips = up.shape[0]
    r = rows((strips, 1))
    even = r % 2 == 0
    x = jnp.where(even, up[...], down[...])
    mirror = bf16(jnp.where(lanes((height, height)) + rows((height, height)) == height - 1, 1.0, 0.0))
    mirrored = jnp.dot(
        split(x), jnp.concatenate([mirror, mirror], axis=0), preferred_element_type=F32
    )
    turning = jnp.where(even, turns[0:1, 2:3], turns[0:1, 3:4])
    x = jnp.where(turning % 2 == 1, mirrored, x)
    cosine, sine = turn_of(turning)
    field = r % (2 * fields) // 2
    u = cosine * x - sine * pltpu.roll(x, strips - 2, 0)
    v = sine * pltpu.roll(x, 2, 0) + cosine * x
    x = jnp.where(field == 2, u, jnp.where(field == 3, v, x))
    cols_o[...] = jnp.transpose(
        jnp.concatenate([x, jnp.zeros((128 - strips, height), F32)], axis=0)
    )


def tables_kernel(dims, sten, cw, token, coefs, shift, spots, cw_v, sem):
    del token
    vectors, levels, fields, height = dims
    per = levels * fields
    copy = pltpu.make_async_copy(cw, cw_v, sem)
    copy.start()
    row, lane = rows((128, 256)), lanes((128, 256))
    move = bf16(jnp.where((lane == row + 1) & (row < 127) | (lane == row + 127) & (row > 0), 1.0, 0.0))
    shift[0:128] = move
    shift[128:256] = move
    source = row % (2 * per)
    for q in range(per):
        hit = (source == 2 * q) & (lane == 0) | (source == 2 * q + 1) & (lane == 255)
        spot = bf16(jnp.where(hit & (row < 2 * per * vectors), 1.0, 0.0))
        spots[q, 0:128] = spot
        spots[q, 128:256] = spot
    one = jnp.ones((1, 128), F32)
    lane = lanes((height, 128))
    for l in range(levels):
        coefs[0, l] = bf16(jnp.concatenate([one, sten[1, l].astype(F32)[:-1]], axis=0))
        coefs[1, l] = bf16(jnp.concatenate([sten[2, l].astype(F32)[1:], one], axis=0))
        right = jnp.dot(sten[3, l], move[:, 0:128], preferred_element_type=F32)
        left = jnp.dot(sten[4, l], move[:, 128:256], preferred_element_type=F32)
        coefs[2, l] = bf16(jnp.where(lane == 0, 1.0, right))
        coefs[3, l] = bf16(jnp.where(lane == 127, 1.0, left))
    copy.wait()


def final_kernel(
    dims, part, kry, adj, sten, coefs, shift, spots, cw, fwd, back, cols, mine, other,
    out_hbm, comb, low, edges, moved, out, sem,
):
    vectors, levels, fields, height = dims
    half = vectors // 2
    per = levels * fields
    total = jnp.broadcast_to(jnp.sum(part[...], axis=1, keepdims=True), (8, 128))
    mix = [jnp.broadcast_to(total[j : j + 1], (8, 128)) for j in range(vectors)]
    is_low = lax.axis_index("lev") & 1 == 0
    mine_mix = [jnp.where(is_low, mix[k], mix[half + k]) for k in range(half)]
    other_mix = [jnp.where(is_low, mix[half + k], mix[k]) for k in range(half)]

    def times(m, x):
        return (x.reshape(-1, 8, 128) * m).reshape(x.shape)

    rim_f = sum(times(mix[k], fwd[k * 16 : (k + 1) * 16]) for k in range(vectors))
    rim_b = sum(times(mix[k], back[k * 16 : (k + 1) * 16]) for k in range(vectors))
    for q in range(per):
        comb[q, 7:8] = rim_f[q : q + 1]
        comb[q, 8 + height : 9 + height] = rim_b[q : q + 1]

    lane = lanes((8, 128)) // (2 * per)
    weight = jnp.zeros((8, 128), F32)
    for k in range(vectors):
        weight = jnp.where(lane == k, mix[k], weight)
    step = 64
    for i in range(height // step):
        edges[i * step : (i + 1) * step] = split(times(weight, cols[i * step : (i + 1) * step]))

    def combine(l, f):
        for i in range(height // step):
            at = slice(i * step, (i + 1) * step)
            comb[l * fields + f, 8 + i * step : 8 + (i + 1) * step] = sum(
                times(mix[k], kry[k, l, f, at].astype(F32)) for k in range(vectors)
            )

    def column(l):
        for c, f in ((0, 0), (1, 3)):
            for i in range(height // step):
                at = slice(i * step, (i + 1) * step)
                if l == levels - 1:
                    x = 0.0
                    for k in range(half):
                        start = (k * 2 + c) * height + i * step
                        x = x + (
                            times(mine_mix[k], mine[start : start + step])
                            + times(other_mix[k], other[start : start + step])
                        )
                else:
                    x = low[c, at]
                low[c, at] = x + comb[l * fields + f, 8 + i * step : 8 + (i + 1) * step]

    def move(l, f):
        q = l * fields + f
        x = comb[q, 8 : 8 + height]
        moved[f] = jnp.dot(split(x), shift[...], preferred_element_type=F32) + jnp.dot(
            edges[...], spots[q], preferred_element_type=F32
        )

    copies = []

    def stencil(l):
        size, block = 32, 64
        for i in range(height // size):
            at = slice(i * size, (i + 1) * size)
            first = 8 + i * size
            c0 = sten[0, l, at].astype(F32)
            c1, c2, c3, c4 = (coefs[d, l, at].astype(F32) for d in range(4))
            for f in range(fields):
                q = l * fields + f
                image = (
                    c0 * comb[q, first : first + size]
                    + c1 * comb[q, first - 1 : first + size - 1]
                    + c2 * comb[q, first + 1 : first + size + 1]
                    + c3 * moved[f, at, 0:128]
                    + c4 * moved[f, at, 128:256]
                )
                if f in (1, 4):
                    c = 0 if f == 1 else 1
                    image = image + cw[c, l, at] * low[c, at]
                out[l, f, at] = adj[l, f, at] + image
            if (i + 1) * size % block == 0:
                n = (i + 1) * size // block - 1
                at = slice(n * block, (n + 1) * block)
                copy = pltpu.make_async_copy(
                    out.at[l, :, at], out_hbm.at[l, :, at], sem.at[len(copies)]
                )
                copy.start()
                copies.append(copy)

    for l in reversed(range(levels)):
        for f in range(fields):
            combine(l, f)
        column(l)
        for f in range(fields):
            move(l, f)
        stencil(l)
    for copy in copies:
        copy.wait()


def final_scratch(dims):
    _, levels, fields, height = dims
    return [
        pltpu.VMEM((levels * fields, height + 16, 128), F32),
        pltpu.VMEM((2, height, 128), F32),
        pltpu.VMEM((height, 256), jnp.bfloat16),
        pltpu.VMEM((fields, height, 256), F32),
        pltpu.VMEM((levels, fields, height, 128), F32),
        pltpu.SemaphoreType.DMA((levels * height // 64,)),
    ]


def pair_kernel(pack, got, o):
    o[...] = pack[-8:] + got[-8:]


def segment_kernel(got, mine, token, held, o):
    del token, held
    o[...] = mine[...] + got[0 : o.shape[0]]


def join_kernel(a, b, near, held, o):
    del near, held
    o[0:8] = a[...] + b[...]


def add_kernel(a, b, *rest):
    o = rest[-1]
    o[...] = a[0:8] + b[0:8]


def keep_kernel(x, token, held, o):
    del token, held
    o[...] = x[...]


def after(x, token, held):
    return local(
        keep_kernel,
        "after",
        6,
        pltpu.VMEM(x.shape, F32),
        [IN_VMEM] * 3,
        *map(pinned, (x, token, held)),
    )


def below_kernel(group_bits, got, mine, token, held, *refs):
    del token, held
    above, (send_o, mine_o) = refs[:-2], refs[-2:]
    group = lax.axis_index("lev")
    upper = group & 1 == 1
    split = mine.shape[0]
    step = 256

    def body(i, carry):
        at = pl.ds(pl.multiple_of(i * step, step), step)
        x = jnp.zeros((step, 128), F32)
        for bit, ref in zip(group_bits, above, strict=True):
            x = x + jnp.where(group & bit == 0, ref[at], 0.0)
        send_o[at] = x + jnp.where(upper, mine[at], 0.0)
        mine_o[at] = x + jnp.where(upper, 0.0, got[at])
        return carry

    lax.fori_loop(0, split // step, body, 0)


def local(kernel, name, us, out_shape, in_specs, *args, limit=SMALL, **more):
    return pl.pallas_call(
        kernel,
        out_shape=out_shape,
        in_specs=in_specs,
        out_specs=jax.tree.map(lambda _: IN_VMEM, out_shape),
        compiler_params=pltpu.CompilerParams(vmem_limit_bytes=limit),
        cost_estimate=pl.CostEstimate(
            flops=int(us * 1e9), bytes_accessed=int(us * 3.5e6), transcendentals=0
        ),
        name=name,
        **more,
    )(*args)


def add(a, b, *held):
    return local(
        add_kernel, "add", 6, pltpu.VMEM((8, 128), F32), [IN_VMEM] * (2 + len(held)),
        *map(pinned, (a, b, *held)),
    )


def per_device(krylov, adjoint, projected, stencil, column_weight, seam_turns):
    vectors, levels, fields, height, width = krylov.shape
    dims = (vectors, levels, fields, height)
    half, per = vectors // 2, levels * fields
    tiles, groups = lax.axis_size("tile"), lax.axis_size("lev")
    count = levels * fields * height * width * tiles * groups
    total_rows = vectors * height
    bf = krylov.dtype
    dma = pltpu.SemaphoreType.DMA

    kry, pack, mine, adj = local(
        functools.partial(dots_kernel, dims, count),
        "dots",
        2,
        (
            pltpu.VMEM(krylov.shape, bf),
            pltpu.VMEM((total_rows + 8, width), F32),
            pltpu.VMEM((total_rows, width), F32),
            pltpu.VMEM(adjoint.shape, F32),
        ),
        [IN_HBM] * 3,
        *map(in_hbm, (projected, krylov, adjoint)),
        scratch_shapes=[
            pltpu.VMEM(projected.shape, F32),
            pltpu.VMEM((vectors, 8, 128), F32),
            dma((fields,)),
            dma((fields,)),
            dma,
        ],
    )
    sten, near, far, cols = local(
        functools.partial(strips_kernel, dims),
        "strips",
        1.5,
        (
            pltpu.VMEM(stencil.shape, bf),
            pltpu.VMEM((vectors * 16 + 8, width), F32),
            pltpu.VMEM((vectors * 16, width), F32),
            pltpu.VMEM((2 * vectors * per, height), F32),
        ),
        [IN_VMEM, IN_HBM],
        pinned(kry),
        in_hbm(stencil),
        scratch_shapes=[pltpu.VMEM((height, width), F32), dma],
    )

    first = exchange(pack, "lev", 1)
    part = local(
        pair_kernel, "pair", 0.1, pltpu.VMEM((8, width), F32), [IN_VMEM] * 2, pinned(pack), pinned(first)
    )
    segment = local(
        segment_kernel,
        "segment",
        6,
        pltpu.VMEM(mine.shape, F32),
        [IN_VMEM] * 4,
        *map(pinned, (first, mine, part, kry)),
    )
    above = []
    for bit in bits("lev")[1:]:
        if above:
            segment = segment + above[-1]
        above.append(exchange(segment, "lev", bit))
    cols = after(cols, part, kry)
    up = shifted(cols, "tile", STRIDE)
    down = up if (2 * STRIDE) % tiles == 0 else shifted(cols, "tile", -STRIDE)

    for bit in bits("lev")[1:-1]:
        part = add(part, exchange(part, "lev", bit))
    coefs, shift, spots, cw = local(
        functools.partial(tables_kernel, dims),
        "tables",
        1.5,
        (
            pltpu.VMEM((4,) + stencil.shape[1:], bf),
            pltpu.VMEM((256, 256), bf),
            pltpu.VMEM((per, 256, 256), bf),
            pltpu.VMEM(column_weight.shape, F32),
        ),
        [IN_VMEM, IN_HBM, IN_VMEM],
        pinned(sten),
        in_hbm(column_weight),
        pinned(part),
        scratch_shapes=[dma],
    )
    got = exchange(part, "lev", bits("lev")[-1])
    near = local(
        join_kernel,
        "join",
        6,
        pltpu.VMEM(near.shape, F32),
        [IN_VMEM] * 4,
        *map(pinned, (part, got, near, shift)),
        input_output_aliases={2: 0},
    )
    far = after(far, near, kry)
    got = exchange(near, "tile", 1)
    part = add(near, got)
    near = got
    far = lax.ppermute(
        far, "tile", [(i, (i + 1 if i % 2 else i - 1) % tiles) for i in range(tiles)]
    )
    for bit in bits("tile")[1:-1]:
        part = add(part, exchange(part, "tile", bit))
    token = part
    send, mine = local(
        functools.partial(below_kernel, bits("lev")[1:]),
        "below",
        6,
        (pltpu.VMEM(mine.shape, F32), pltpu.VMEM(mine.shape, F32)),
        [IN_VMEM] * (4 + len(above)),
        *map(pinned, (first, mine, token, kry, *above)),
    )
    other = exchange(send, "lev", 1)

    fwd, back, cols = local(
        functools.partial(turn_kernel, dims),
        "turn",
        1,
        (
            pltpu.VMEM(far.shape, F32),
            pltpu.VMEM(far.shape, F32),
            pltpu.VMEM((height, width), F32),
        ),
        [IN_VMEM] * 5,
        *map(pinned, (seam_turns, near, far, up, down)),
    )

    for bit in bits("tile")[-1:]:
        part = add(part, exchange(part, "tile", bit))

    return pl.pallas_call(
        functools.partial(final_kernel, dims),
        out_shape=jax.ShapeDtypeStruct(adjoint.shape, F32),
        in_specs=[IN_VMEM] * 13,
        out_specs=IN_HBM,
        scratch_shapes=final_scratch(dims),
        compiler_params=pltpu.CompilerParams(vmem_limit_bytes=LARGE),
        name="final",
    )(
        *map(
            pinned,
            (part, kry, adj, sten, coefs, shift, spots, cw, fwd, back, cols, mine, other),
        )
    )


def solution(mesh):
    placed = (
        P(None, "lev", None, "tile", None),
        P("lev", None, "tile", None),
        P(),
        P(None, "lev", "tile", None),
        P(None, "lev", "tile", None),
        P("tile", None),
    )
    return jax.shard_map(
        per_device,
        mesh=mesh,
        in_specs=placed,
        out_specs=P("lev", None, "tile", None),
        check_vma=False,
    )
```
